32 devices in a mesh: dp: 4 (over x, core), expert: 8 (over z, y).
Axes of the slice: x: 2, y: 2, z: 4, core: 2. Of those that a mesh axis runs over, the one named last changes fastest.
Arguments:
- block_input: bfloat16 [8192, 768], P(('dp', 'expert')), may hold values from -6 to 6
- gain_attn: float32 [768], replicated, may hold values from 0.1 to 1.9
- w_qkv: bfloat16 [768, 2304], replicated, may hold values from -0.21875 to 0.21875
- w_mix: bfloat16 [768, 768], replicated, may hold values from -0.875 to 0.875
- rel_bias: float32 [32, 12], replicated, may hold values from -4 to 4
- gain_ffn: float32 [768], replicated, may hold values from 0.1 to 1.9
- w_router: float32 [768, 8], replicated, may hold values from -0.15625 to 0.15625
- w_up: bfloat16 [8, 768, 3072], P('expert', None, 'dp'), may hold values from -0.21875 to 0.21875
- w_down: bfloat16 [8, 768, 3072], P('expert', None, 'dp'), may hold values from -0.15625 to 0.15625
- routes: int32 [8192, 2], P(('dp', 'expert')), may hold values from 0 to 7, all different within a row
- fill_order: int32 [32, 512], P(('dp', 'expert')), may hold values from 0 to 511, each once within a row
- grad_output: bfloat16 [8192, 768], P(('dp', 'expert')), may hold values from -6 to 6
Outputs:
- output: bfloat16 [8192, 768], P(('dp', 'expert'))
- grad_input: float32 [8192, 768], P(('dp', 'expert'))
- grad_gain_attn: float32 [768], replicated
- grad_w_qkv: float32 [768, 2304], replicated
- grad_w_mix: float32 [768, 768], replicated
- grad_rel_bias: float32 [32, 12], replicated
- grad_gain_ffn: float32 [768], replicated
- grad_router: float32 [768, 8], replicated
- grad_w_up: float32 [8, 768, 3072], P('expert', None, 'dp')
- grad_w_down: float32 [8, 768, 3072], P('expert', None, 'dp')
The draws below stay inside these ranges and needn't reach their ends.
Inputs may be any that keep to these rules, and one draw needn't show every extreme that they name: `routes`: each row names two different experts. `fill_order`: each row holds every number from 0 to 511 once.
All inputs are finite; a program needn't handle non-finite values.
Results may differ from the reference program's by a relative error of at most 0.018.
Values may be sent and summed in bfloat16 or wider, within the bound.
No kernel may reach another device: no remote copies, remote signals or barrier semaphores. Data moves between devices by JAX's collectives and lax.ppermute only.
A program may use at most 192 MiB of HBM per device.

```python
import math
import jax
import jax.numpy as jnp
from jax import lax

D = 768
HEADS = 12
HDIM = 64
FF = 3072
BUCKETS = 32
CLEN = 128
P_DEV = 128
EXPERTS = 8
TOK_DEV = 256
PROMPT = 512
TOKENS = 8192
CAP = 72
N_DP = 4
N_EXPERT = 8


def shard_levels(stream_key, dims, cuts, least, top_value):
    factor_of, own = 1.0, jax.random.fold_in(stream_key, 6)
    for position, blocks in cuts:
        steps = jnp.exp(jax.random.uniform(jax.random.fold_in(own, position), (blocks,), jnp.float32, least / len(cuts), top_value / len(cuts)))
        factor_of = factor_of * jnp.repeat(steps, dims[position] // blocks).reshape([-1 if axis == position else 1 for axis in range(len(dims))])
    return factor_of


def choose_distinct(stream_key, rows, amount, top, lift):
    sequence = jax.random.permutation(jax.random.fold_in(stream_key, 1), amount)
    pull = sequence
    for power in range(3):
        pull = pull * pull // amount
    pull = pull * lift // amount
    lots = jax.random.randint(jax.random.fold_in(stream_key, 2), (rows, amount), 0, 4096) + pull
    fixed_rows = jax.random.permutation(jax.random.fold_in(stream_key, 3), rows)[jnp.arange(amount) % rows]
    lots = jnp.where(jnp.arange(rows)[:, None] == fixed_rows[None, :], 1 << 14, lots)
    merit = lots * amount + jnp.arange(amount)
    return lax.top_k(merit.astype(jnp.int32), top)[1].astype(jnp.int32)


def noise(rng, shape, scale, most, shards=(), kind=jnp.bfloat16):
    array = scale * jax.random.normal(rng, shape, jnp.float32)
    if shards:
        array = array * shard_levels(rng, shape, shards, -0.22, 0.18)
    return jnp.clip(array, -most, most).astype(kind)


def setup_inputs(seed: int = 0) -> dict:
    seeds = jax.random.split(jax.random.key(seed), 13)
    return {
        "block_input": noise(seeds[0], (TOKENS, D), 1.0, 6.0, ((0, 32),)),
        "gain_attn": jnp.clip(1.0 + 0.18 * jax.random.normal(seeds[1], (D,), jnp.float32), 0.1, 1.9),
        "w_qkv": noise(seeds[2], (D, 3 * D), D ** -0.5, 0.21875),
        "w_mix": noise(seeds[3], (D, D), (D // 16) ** -0.5, 0.875),
        "rel_bias": noise(seeds[4], (BUCKETS, HEADS), 1.0, 4.0, (), jnp.float32),
        "gain_ffn": jnp.clip(1.0 + 0.18 * jax.random.normal(seeds[5], (D,), jnp.float32), 0.1, 1.9),
        "w_router": noise(seeds[6], (D, EXPERTS), (2 * D) ** -0.5, 0.15625, (), jnp.float32),
        "w_up": noise(seeds[7], (EXPERTS, D, FF), D ** -0.5, 0.21875, ((0, 8), (2, 4))),
        "w_down": noise(seeds[8], (EXPERTS, D, FF), (FF // 2) ** -0.5, 0.15625, ((0, 8), (2, 4))),
        "routes": choose_distinct(seeds[9], TOKENS, EXPERTS, 2, 4096),
        "fill_order": jax.vmap(lambda own: jax.random.permutation(own, 2 * TOK_DEV))(jax.random.split(seeds[10], (N_DP * N_EXPERT))).reshape((N_DP * N_EXPERT, 2 * TOK_DEV)).astype(jnp.int32),
        "grad_output": noise(seeds[11], (TOKENS, D), 1.0, 6.0, ((0, 32),)),
    }


@jax.custom_vjp
def low(v):
    return lax.optimization_barrier(v.astype(jnp.bfloat16)).astype(jnp.float32)

@jax.custom_vjp
def low_back(v):
    return v

def low_keep(v):
    return (low(v), None)

def low_pass(kept, grad):
    return (grad,)

def back_keep(v):
    return (v, None)

def back_low(kept, grad):
    return (low(grad),)
low.defvjp(low_keep, low_pass)
low_back.defvjp(back_keep, back_low)
epsilon = 1e-06
masked_score = -1e+30
bucket_edges = [int(math.ceil(16 * 8 ** (step / 16))) for step in range(1, 16)]
highest = lax.Precision.HIGHEST

def rms_norm(values, gain):
    return values * lax.rsqrt(lax.optimization_barrier(jnp.mean(values * values, axis=-1, keepdims=True)) + epsilon) * gain

def bucket_of(distance):
    beyond = sum(((distance >= edge).astype(jnp.int32) for edge in bucket_edges))
    return jnp.where(distance < 16, distance, 16 + beyond)

def slot_plan(device_routes, device_order):
    pair_expert = device_routes.reshape(-1)
    same = pair_expert[:, None] == pair_expert[None, :]
    before = device_order[None, :] < device_order[:, None]
    rank = lax.optimization_barrier(jnp.sum((same & before).astype(jnp.int32), axis=1))
    kept = rank < CAP
    slot_id = jnp.where(kept, pair_expert * CAP + rank, EXPERTS * CAP)
    pair_token = jnp.arange(2 * TOK_DEV, dtype=jnp.int32) // 2
    slot_token = jnp.zeros((EXPERTS * CAP,), jnp.int32).at[slot_id].set(pair_token, mode='drop')
    slot_used = jnp.zeros((EXPERTS * CAP,), jnp.bool_).at[slot_id].set(True, mode='drop')
    return (kept, jnp.minimum(slot_id, EXPERTS * CAP - 1), slot_token, slot_used)

def attend_device(grid, table, index):
    row = index // N_EXPERT
    group = index % N_EXPERT
    member = lax.dynamic_index_in_dim(grid, group, axis=1, keepdims=False)
    prompt_pairs = member[:, :P_DEV, D:].reshape(PROMPT, 2 * D)
    own = lax.dynamic_index_in_dim(member, row, axis=0, keepdims=False)
    pairs = jnp.concatenate([prompt_pairs, own[P_DEV:, D:]], axis=0)
    query_pos = jnp.concatenate([row * P_DEV + jnp.arange(P_DEV, dtype=jnp.int32), PROMPT + jnp.arange(CLEN, dtype=jnp.int32)])
    key_pos = jnp.concatenate([jnp.arange(PROMPT, dtype=jnp.int32), PROMPT + jnp.arange(CLEN, dtype=jnp.int32)])
    queries = own[:, :D].reshape(TOK_DEV, HEADS, HDIM)
    keys = pairs[:, :D].reshape(PROMPT + CLEN, HEADS, HDIM)
    values = pairs[:, D:].reshape(PROMPT + CLEN, HEADS, HDIM)
    scores = jnp.einsum('qhe,khe->hqk', queries, keys, precision=highest) * HDIM ** (-0.5)
    distance = query_pos[:, None] - key_pos[None, :]
    buckets = jnp.clip(bucket_of(distance), 0, BUCKETS - 1)
    scores = scores + jnp.transpose(table[buckets], (2, 0, 1))
    scores = low_back(scores)
    allowed = (distance >= 0)[None]
    scores = jnp.where(allowed, scores, masked_score)
    top = lax.optimization_barrier(jnp.max(scores, axis=-1, keepdims=True))
    total = lax.optimization_barrier(jnp.sum(jnp.where(allowed, jnp.exp(scores - top), 0.0), axis=-1, keepdims=True))
    chances = jnp.where(allowed, jnp.exp(scores - (top + jnp.log(total))), 0.0)
    attended = jnp.einsum('hqk,khe->qhe', low(chances), values, precision=highest)
    return attended.reshape(TOK_DEV, D)

def expert_apply(rows, up_weight, down_weight):
    pre_act = low_back(jnp.dot(rows, up_weight, precision=highest))
    active = low(jax.nn.gelu(pre_act, approximate=True))
    return low(low_back(jnp.dot(active, down_weight.T, precision=highest)))

def reference(block_input, gain_attn, w_qkv, w_mix, rel_bias, gain_ffn, w_router, w_up, w_down, routes, fill_order, grad_output):
    device_count = N_DP * N_EXPERT
    kept, slot_safe, slot_token, slot_used = jax.vmap(slot_plan)(routes.reshape(device_count, TOK_DEV, 2), fill_order)

    def forward(inputs, gain_one, weight_qkv, weight_mix, table, gain_two, router, up_all, down_all):
        normed = rms_norm(inputs, gain_one)
        normed_low = low(normed)
        projected = low(low_back(jnp.dot(normed_low, weight_qkv, precision=highest)))
        grid = projected.reshape(N_DP, N_EXPERT, TOK_DEV, 3 * D)
        attend_saved = jax.checkpoint(attend_device)
        attended = lax.map(lambda index: attend_saved(grid, table, index), jnp.arange(device_count, dtype=jnp.int32))
        attended_low = low(low_back(attended.reshape(TOKENS, D)))
        hidden = inputs + low_back(jnp.dot(attended_low, weight_mix, precision=highest))
        normed_two = rms_norm(hidden, gain_two)
        chance_row = jax.nn.softmax(jnp.dot(normed_two, router, precision=highest), axis=-1)
        picked = jnp.take_along_axis(chance_row, routes, axis=1)
        gates = picked / lax.optimization_barrier(jnp.sum(picked, axis=1, keepdims=True))
        normed_two_low = low(normed_two)
        outgoing = jax.vmap(lambda rows, tokens, used: jnp.where(used[:, None], rows[tokens], 0.0))(normed_two_low.reshape(device_count, TOK_DEV, D), slot_token, slot_used)
        expert_rows = outgoing.reshape(N_DP, N_EXPERT, EXPERTS, CAP, D).transpose(2, 0, 1, 3, 4).reshape(EXPERTS, N_DP * N_EXPERT * CAP, D)
        expert_rows = low_back(expert_rows)
        apply_saved = jax.checkpoint(expert_apply)
        results = lax.map(lambda packed: apply_saved(packed[0], packed[1], packed[2]), (expert_rows, up_all, down_all))
        returned = results.reshape(EXPERTS, N_DP, N_EXPERT, CAP, D).transpose(1, 2, 0, 3, 4).reshape(device_count, EXPERTS * CAP, D)
        pair_out = jax.vmap(lambda back, slot, keep: jnp.where(keep[:, None], back[slot], 0.0))(returned, slot_safe, kept)
        pair_out = pair_out.reshape(TOKENS, 2, D)
        return hidden + lax.optimization_barrier(jnp.sum(gates[..., None] * pair_out, axis=1))
    floats = (block_input.astype(jnp.float32), gain_attn, w_qkv.astype(jnp.float32), w_mix.astype(jnp.float32), rel_bias, gain_ffn, w_router, w_up.astype(jnp.float32), w_down.astype(jnp.float32))
    output, pullback = jax.vjp(forward, *floats)
    grads = pullback(grad_output.astype(jnp.float32))
    return (output.astype(jnp.bfloat16), grads[0], grads[1], grads[2], grads[3], grads[4], grads[5], grads[6], grads[7], grads[8])
```

```python
import functools
import math

import jax
import jax.numpy as jnp
from jax import lax
from jax.experimental import pallas as pl
from jax.experimental.pallas import tpu as pltpu
from jax.sharding import PartitionSpec as P

CLEN = 128
P_DEV = 128

epsilon = 1e-06
masked_score = -1e30
bucket_edges = [int(math.ceil(16 * 8 ** (step / 16))) for step in range(1, 16)]
bf16 = jnp.bfloat16
f32 = jnp.float32
highest = lax.Precision.HIGHEST
VMEM = pl.BlockSpec(memory_space=pltpu.VMEM)
SMEM = pl.BlockSpec(memory_space=pltpu.SMEM)


def dot(left, right, precision=None):
    return lax.dot_general(
        left, right, (((1,), (0,)), ((), ())), precision=precision, preferred_element_type=f32
    )


def dot_cols(left, right, precision=None):
    return lax.dot_general(
        left, right, (((1,), (1,)), ((), ())), precision=precision, preferred_element_type=f32
    )


def dot_rows(left, right, precision=None):
    return lax.dot_general(
        left, right, (((0,), (0,)), ((), ())), precision=precision, preferred_element_type=f32
    )


def iota(shape, axis):
    return lax.broadcasted_iota(jnp.int32, shape, axis)


def call(kernel, outs, scratch, args, flops, limit, smem=1):
    size = sum(a.size * a.dtype.itemsize for a in args) + sum(
        math.prod(o.shape) * o.dtype.itemsize for o in outs
    )
    return pl.pallas_call(
        kernel,
        out_shape=outs,
        in_specs=[SMEM] * smem + [VMEM] * (len(args) - smem),
        out_specs=[VMEM] * len(outs),
        scratch_shapes=scratch,
        compiler_params=pltpu.CompilerParams(vmem_limit_bytes=limit * 1024 * 1024),
        cost_estimate=pl.CostEstimate(flops=flops, bytes_accessed=size, transcendentals=0),
    )(*args)


def like(shape, dtype):
    return jax.ShapeDtypeStruct(shape, dtype)


def bucket_of(distance):
    beyond = sum(((distance >= edge).astype(jnp.int32) for edge in bucket_edges))
    return jnp.clip(jnp.where(distance < 16, distance, 16 + beyond), 0, 31)


def thirds(value):
    high = value.astype(bf16).astype(f32)
    mid = (value - high).astype(bf16).astype(f32)
    return high, mid, value - high - mid


def norm_rows(values):
    return lax.rsqrt(jnp.mean(values * values, axis=-1, keepdims=True) + epsilon)


def route_kernel(experts, cap, rows, place, routes, fill_order, grad_out, pos_c, pos_r, sent):
    count = routes.shape[1]
    me = place[0]
    order = jnp.broadcast_to(fill_order[...], (16, 2 * count))
    coarse = order & ~31
    order = jnp.where(iota(order.shape, 0) < 8, coarse, order - coarse).astype(f32).astype(bf16)
    at, to = iota((2 * count, 2 * count), 0), iota((2 * count, 2 * count), 1)
    pick = (at == jnp.where(to < count, 2 * to, 2 * (to - count) + 1)).astype(f32).astype(bf16)
    order = dot(order, pick)
    order = order[:8] + order[8:]
    orow = [order[:1, :count], order[:1, count:]]
    row = [routes[c : c + 1, :].astype(f32) for c in range(2)]
    lines = jnp.concatenate([*row, *orow, jnp.zeros((4, count), f32)], axis=0)
    lines = jnp.transpose(lines)
    col = [lines[:, c : c + 1] for c in range(2)]
    ocol = [lines[:, c : c + 1] for c in range(2, 4)]
    slots = []
    for c in range(2):
        rank_c = jnp.zeros((count, 1), f32)
        rank_r = jnp.zeros((1, count), f32)
        for other in range(2):
            hit = (col[c] == row[other]) & (orow[other] < ocol[c])
            rank_c += jnp.sum(hit.astype(f32), axis=1, keepdims=True)
            hit = (col[other] == row[c]) & (ocol[other] < orow[c])
            rank_r += jnp.sum(hit.astype(f32), axis=0, keepdims=True)
        rank_c = rank_c.astype(jnp.int32)
        rank_r = rank_r.astype(jnp.int32)
        slot = (col[c].astype(jnp.int32) ^ me) * rows + rank_c
        pos_c[:, c : c + 1] = jnp.where(rank_c < cap, slot, -1)
        slot = (routes[c : c + 1, :] ^ me) * rows + rank_r
        slots.append(jnp.where(rank_r < cap, slot, -1))
        pos_r[c : c + 1, :] = slots[c]
    grad_top = grad_out[...]
    for k in range(experts):
        index = iota((rows, count), 0) + k * rows
        onehot = ((index == slots[0]) | (index == slots[1])).astype(f32).astype(bf16)
        sent[k ^ me] = dot(onehot, grad_top).astype(bf16)


def project_kernel(x, gain, w_qkv, table, normed_low, projected, tiles):
    values = x[...].astype(f32)
    low = (values * norm_rows(values) * gain[...]).astype(bf16)
    normed_low[...] = low
    projected[...] = dot(low, w_qkv[...]).astype(bf16)
    buckets, heads = table.shape
    width = 2 * P_DEV
    onehot = (bucket_of(iota((buckets, width), 1)) == iota((buckets, width), 0)).astype(f32)
    line = dot_rows(table[...], onehot, highest)
    causal = iota((P_DEV, P_DEV), 1) >= iota((P_DEV, P_DEV), 0)
    for h in range(heads):
        spread = jnp.broadcast_to(line[h : h + 1, :], (P_DEV, width))
        rolled = pltpu.roll(spread, 0, 1, stride=1, stride_axis=0)
        tiles[h, 0] = jnp.full((P_DEV, P_DEV), masked_score, f32)
        tiles[h, 1] = jnp.where(causal, rolled[:, :P_DEV], masked_score)
        tiles[h, 2] = rolled[:, P_DEV:]
        tiles[h, 3] = jnp.broadcast_to(line[h : h + 1, width - 1 : width], (P_DEV, P_DEV))


def tile_index(block, dp_size, dp_index, continuation):
    if block == 0:
        return 1 if continuation else 0
    key = dp_index ^ (block - 1)
    if continuation:
        return jnp.minimum(dp_size - key, 2) + 1
    if block == 1:
        return 1
    return jnp.clip(dp_index - key, -1, 2) + 1


def attend_kernel(dp_size, heads, cap, rows, experts, place, x, projected, gain, w_qkv, tiles,
                  w_mix, gain_ffn, w_router, routes_c, pos_c, pos_r, *rest):
    others = rest[: dp_size - 1]
    (hidden, attended, gates, chances, pairs, normed_others, *sent) = rest[dp_size - 1 : -1]
    scores = rest[-1]
    count, width = x.shape
    head_size = width // heads
    keys = (dp_size + 1) * P_DEV
    dp_index = place[1]
    values = jnp.concatenate([o[...] for o in others], axis=0).astype(f32)
    low = (values * norm_rows(values) * gain[...]).astype(bf16)
    normed_others[...] = low
    pairs[0:CLEN, :] = projected[P_DEV:, width:]
    pairs[CLEN : 2 * CLEN, :] = projected[:P_DEV, width:]
    pairs[2 * CLEN :, :] = dot(low, w_qkv[:, width:]).astype(bf16)
    left = iota((count, P_DEV), 1) < head_size
    for p in range(heads // 2):
        cut = slice(p * P_DEV, (p + 1) * P_DEV)
        key = pairs[:, cut]
        value_t = jnp.transpose(pairs[:, width + p * P_DEV : width + (p + 1) * P_DEV])
        query = projected[:, cut] * bf16(head_size**-0.5)
        zero = jnp.zeros_like(query)
        parts = []
        for s in range(2):
            h = 2 * p + s
            part = jnp.where(left, query, zero) if s == 0 else jnp.where(left, zero, query)
            raw = dot_cols(key, part)
            top = None
            for b in range(dp_size + 1):
                bias = jnp.concatenate(
                    [
                        tiles[h, tile_index(b, dp_size, dp_index, False)],
                        tiles[h, tile_index(b, dp_size, dp_index, True)],
                    ],
                    axis=1,
                )
                block = raw[b * P_DEV : (b + 1) * P_DEV, :] + bias
                scores[s, b * P_DEV : (b + 1) * P_DEV, :] = block
                most = jnp.max(block, axis=0, keepdims=True)
                top = most if top is None else jnp.maximum(top, most)
            total = jnp.zeros((1, count), f32)
            for b in range(dp_size + 1):
                weight = jnp.exp(scores[s, b * P_DEV : (b + 1) * P_DEV, :] - top)
                scores[s, b * P_DEV : (b + 1) * P_DEV, :] = weight
                total += jnp.sum(weight, axis=0, keepdims=True)
            inverse = 1.0 / total
            chances[h, :, :] = (scores[s] * inverse).astype(bf16)
            parts.append(dot(value_t[s * head_size : (s + 1) * head_size, :], chances[h]))
        attended[:, cut] = jnp.transpose(jnp.concatenate(parts, axis=0))
    hid = x[...].astype(f32) + dot(attended[...].astype(bf16), w_mix[...])
    hidden[...] = hid
    normed_two = hid * norm_rows(hid) * gain_ffn[...]
    logits = dot(normed_two, w_router[...], highest)
    lane = iota(logits.shape, 1)
    pick = [
        jnp.sum(jnp.where(lane == routes_c[:, c : c + 1], logits, 0.0), axis=1, keepdims=True)
        for c in range(2)
    ]
    most = jnp.maximum(pick[0], pick[1])
    raised = [jnp.exp(v - most) for v in pick]
    gate = [v / (raised[0] + raised[1]) for v in raised]
    lane = iota((count, P_DEV), 1)
    gates[...] = jnp.where(lane == 0, gate[0], jnp.where(lane == 1, gate[1], 0.0))
    low = normed_two.astype(bf16)
    for k in range(experts):
        index = iota((rows, count), 0) + k * rows
        onehot = (index == pos_r[0:1, :]) | (index == pos_r[1:2, :])
        block = dot(onehot.astype(f32).astype(bf16), low)
        line = jnp.zeros((1, P_DEV), f32)
        for c in range(2):
            mine = pos_c[:, c : c + 1] == lane + k * rows
            line += jnp.sum(jnp.where(mine, gate[c], 0.0), axis=0, keepdims=True)
        line = jnp.concatenate([*thirds(line), jnp.zeros((1, width - 3 * P_DEV), f32)], axis=1)
        sent[k][...] = jnp.where(iota((rows, width), 0) == cap, line, block).astype(bf16)


def gelu_parts(value):
    factor = math.sqrt(2 / math.pi)
    square = value * value
    bend = jnp.tanh(factor * value * (1.0 + 0.044715 * square))
    half = 0.5 * (1.0 + bend)
    slope = half + (0.5 * factor) * value * (1.0 - bend * bend) * (1.0 + 0.134145 * square)
    return value * half, slope


def expert_kernel(experts, cap, rows, place, tops, downs, *refs):
    me, dp_index = place[0], place[1]
    blocks, _, units = downs.shape
    ups, refs = refs[:blocks], refs[blocks:]
    got, refs = refs[:experts], refs[experts:]
    results, backs = refs[:experts], refs[experts : 2 * experts]
    arrived, grad_out, active, grad_pre = refs[2 * experts :]
    width = arrived.shape[1]
    for k in range(experts):
        at = slice(k * rows, (k + 1) * rows)
        block = got[k][...]
        arrived[at, :] = block
        line = block[rows - 16 :, : 3 * P_DEV].astype(f32)[cap - rows + 16 : cap - rows + 17, :]
        line = line[:, :P_DEV] + line[:, P_DEV : 2 * P_DEV] + line[:, 2 * P_DEV :]
        same = iota((rows, P_DEV), 0) == iota((rows, P_DEV), 1)
        gate = jnp.sum(jnp.where(same, line, 0.0), axis=1, keepdims=True)
        grad_out[at, :] = (gate * tops[k ^ me].astype(f32)).astype(bf16)
    chunk = 256 if units % 256 == 0 else 128
    for q in range(blocks):
        for first in range(0, units, chunk):
            at = slice(q * units + first, q * units + first + chunk)
            here = slice(first, first + chunk)
            low, slope = gelu_parts(dot(arrived[...], ups[q][:, here]))
            active[:, at] = low.astype(bf16)
            grad_pre[:, at] = (dot(grad_out[...], downs[q ^ dp_index, :, here]) * slope).astype(bf16)
    result = None
    back = None
    for q in range(blocks):
        at = slice(q * units, (q + 1) * units)
        step = dot_cols(active[:, at], downs[q ^ dp_index])
        result = step if result is None else result + step
        step = dot_cols(grad_pre[:, at], ups[q][...])
        back = step if back is None else back + step
    result = result.astype(bf16)
    for k in range(experts):
        at = slice(k * rows, (k + 1) * rows)
        results[k][...] = result[at]
        gate = jnp.sum(
            result[at].astype(f32) * tops[k ^ me].astype(f32), axis=1, keepdims=True
        )
        same = iota((rows, P_DEV), 0) == iota((rows, P_DEV), 1)
        line = jnp.sum(jnp.where(same, gate, 0.0), axis=0, keepdims=True)
        line = jnp.concatenate([*thirds(line), jnp.zeros((1, width - 3 * P_DEV), f32)], axis=1)
        backs[k][...] = jnp.where(iota((rows, width), 0) == cap, line, back[at]).astype(bf16)


def weight_kernel(place, arrived, grad_out, active, grad_pre, grads):
    blocks, _, _, units = grads.shape
    rows_t = jnp.transpose(arrived[...])
    grad_t = jnp.transpose(grad_out[...])
    for q in range(blocks):
        at = slice(q * units, (q + 1) * units)
        grads[q ^ place[1], 0] = dot(rows_t, grad_pre[:, at]).astype(bf16)
        grads[q ^ place[1], 1] = dot(grad_t, active[:, at]).astype(bf16)


def combine_kernel(experts, rows, hidden, gates, pos_c, *refs):
    back, (output, held) = refs[:experts], refs[experts:]
    count = hidden.shape[0]
    for k in range(experts):
        held[k * rows : (k + 1) * rows, :] = back[k][...]
    index = iota((count, experts * rows), 1)
    total = hidden[...]
    for c in range(2):
        onehot = (index == pos_c[:, c : c + 1]).astype(f32).astype(bf16)
        total += gates[:, c : c + 1] * dot(onehot, held[...])
    output[...] = total.astype(bf16)


def diagonal_sums(values):
    size, width = values.shape
    while size > 8:
        size //= 2
        values = values[:size] + pltpu.roll(values[size:], width - size, 1)
    row = iota(values.shape, 0)
    for bit in (4, 2, 1):
        values = jnp.where((row & bit) != 0, pltpu.roll(values, width - bit, 1), values)
    return jnp.sum(values, axis=0, keepdims=True)


def write_blocks(into, mine, value, small=()):
    blocks, rows, width = into.shape
    step = value.shape[0] // blocks
    for p in range(blocks):
        part = value[p * step : (p + 1) * step]
        if rows > step:
            more = small[p] if p < len(small) else jnp.zeros((8, width), f32)
            part = jnp.concatenate([part, more], axis=0)
        into[p ^ mine] = part.astype(bf16)


def row_zero(line):
    return jnp.where(iota((8, line.shape[1]), 0) == 0, line, 0.0)


def router_kernel(heads, cap, rows, experts, place, hidden, gates, pos_c, routes_c, gain_ffn,
                  w_router, grad_output, attended, w_mix, *rest):
    back = rest[:experts]
    grad_hidden, grad_att, delta, mix, held = rest[experts:]
    count, width = hidden.shape
    head_size = width // heads
    for k in range(experts):
        held[k * rows : (k + 1) * rows, :] = back[k][...]
    index = iota((count, experts * rows), 1)
    onehot = (index == pos_c[:, 0:1]) | (index == pos_c[:, 1:2])
    grad_two = dot(onehot.astype(f32).astype(bf16), held[...])
    lane = iota((count, P_DEV), 1)
    found = [jnp.zeros((count, P_DEV), f32) for c in range(2)]
    for k in range(experts):
        line = back[k][rows - 16 :, : 3 * P_DEV].astype(f32)
        line = line[cap - rows + 16 : cap - rows + 17, :]
        line = line[:, :P_DEV] + line[:, P_DEV : 2 * P_DEV] + line[:, 2 * P_DEV :]
        for c in range(2):
            found[c] += jnp.where(pos_c[:, c : c + 1] == lane + k * rows, line, 0.0)
    grad_gate = [jnp.sum(v, axis=1, keepdims=True) for v in found]
    hid = hidden[...]
    scale = norm_rows(hid)
    normed_two = hid * scale * gain_ffn[...]
    slope = gates[:, 0:1] * gates[:, 1:2] * (grad_gate[0] - grad_gate[1])
    lane = iota((count, w_router.shape[1]), 1)
    grad_logits = jnp.where(lane == routes_c[:, 0:1], slope, 0.0) - jnp.where(
        lane == routes_c[:, 1:2], slope, 0.0
    )
    grad_two += dot_cols(grad_logits, w_router[...], highest)
    grad_router = dot_rows(grad_logits, normed_two, highest)
    grad_gain_ffn = jnp.sum(grad_two * hid * scale, axis=0, keepdims=True)
    weighted = grad_two * gain_ffn[...]
    inner = jnp.mean(weighted * hid, axis=-1, keepdims=True)
    grad_hid = grad_output[...].astype(f32) + scale * weighted - hid * (scale**3 * inner)
    grad_hidden[...] = grad_hid
    mixed = grad_hid.astype(bf16)
    att = attended[...]
    small = [row_zero(grad_gain_ffn)]
    small += [grad_router[i : i + 8] for i in range(0, experts, 8)]
    write_blocks(mix, place[5], dot_rows(att.astype(bf16), mixed), small)
    top = dot_cols(mixed, w_mix[...]).astype(bf16)
    grad_att[...] = top
    prod_t = jnp.transpose(top.astype(f32) * att)
    for h in range(heads):
        delta[h : h + 1, :] = jnp.sum(
            prod_t[h * head_size : (h + 1) * head_size, :], axis=0, keepdims=True
        )


def backward_kernel(dp_size, heads, place, grad_att, delta, chances, pairs, projected,
                    normed_low, normed_others, gain, w_qkv, *rest):
    grad_w, grad_rest, grad_odd, grad_even = rest[:3], *rest[3:5], rest[5:-6]
    sums, grad_query, grad_pairs, normed_t, normed_all, lines = rest[-6:]
    count, width = grad_att.shape
    head_size = width // heads
    dp_index = place[1]
    normed_all[0:CLEN, :] = normed_low[P_DEV:, :]
    normed_all[CLEN : 2 * CLEN, :] = normed_low[:P_DEV, :]
    normed_all[2 * CLEN :, :] = normed_others[...]
    normed_t[...] = jnp.transpose(normed_all[...])
    left = iota((count, P_DEV), 1) < head_size
    left_keys = iota((pairs.shape[0], P_DEV), 1) < head_size
    lines[...] = jnp.zeros_like(lines)
    for p in range(heads // 2):
        cut = slice(p * P_DEV, (p + 1) * P_DEV)
        cut_value = slice(width + p * P_DEV, width + (p + 1) * P_DEV)
        key_t = jnp.transpose(pairs[:, cut])
        value = pairs[:, cut_value]
        query = projected[:, cut] * bf16(head_size**-0.5)
        top = grad_att[:, cut]
        zero = jnp.zeros_like(top)
        grad_q, grad_k, grad_v = [], [], []
        for s in range(2):
            h = 2 * p + s
            part = jnp.where(left, top, zero) if s == 0 else jnp.where(left, zero, top)
            grad_chance = dot_cols(value, part)
            chance = chances[h]
            grad_score = (chance.astype(f32) * (grad_chance - delta[h : h + 1, :])).astype(bf16)
            grad_v.append(dot(chance, top))
            grad_k.append(dot(grad_score, query))
            grad_q.append(dot(key_t[s * head_size : (s + 1) * head_size, :], grad_score))
            sums[...] = jnp.zeros_like(sums)
            for b in range(dp_size + 1):
                tile = grad_score[b * P_DEV : (b + 1) * P_DEV, :].astype(f32)
                if b > 0:
                    sums[tile_index(b, dp_size, dp_index, False)] += tile[:, :P_DEV]
                sums[tile_index(b, dp_size, dp_index, True)] += tile[:, P_DEV:]
            both = jnp.concatenate([sums[1], sums[2]], axis=1)
            lines[h : h + 1, : 2 * P_DEV] = diagonal_sums(both)
            lines[h : h + 1, 2 * P_DEV :] = jnp.sum(sums[3], axis=0, keepdims=True)
        grad_pairs[:, cut] = jnp.where(left_keys, grad_k[0], grad_k[1]).astype(bf16)
        grad_pairs[:, cut_value] = jnp.where(left_keys, grad_v[0], grad_v[1]).astype(bf16)
        grad_q = jnp.transpose(jnp.concatenate(grad_q, axis=0) * head_size**-0.5)
        grad_query[0:CLEN, cut] = grad_q[P_DEV:].astype(bf16)
        grad_query[CLEN:, cut] = grad_q[:P_DEV].astype(bf16)
    grad_low = dot_cols(grad_pairs[...], w_qkv[:, width:])
    own = grad_low[:count] + dot_cols(grad_query[...], w_qkv[:, :width])
    grad_rest[...] = own[:CLEN]
    grad_even[0][...] = own[CLEN:]
    for k in range(1, dp_size):
        into = grad_odd.at[k // 2] if k % 2 else grad_even[k // 2]
        into[...] = grad_low[(k + 1) * P_DEV : (k + 2) * P_DEV].astype(bf16)
    grad_gain = jnp.sum(own * normed_all[:count, :].astype(f32), axis=0, keepdims=True)
    grad_gain += jnp.sum(
        grad_low[count:] * normed_all[count:, :].astype(f32), axis=0, keepdims=True
    )
    grad_gain = grad_gain / gain[...]
    distance = iota((lines.shape[1], P_DEV), 0)
    bucket = jnp.where(distance < 2 * P_DEV, bucket_of(distance), 31)
    onehot = (bucket == iota((lines.shape[1], P_DEV), 1)).astype(f32)
    table = dot(lines[...], onehot, highest)
    table = jnp.concatenate([table, jnp.zeros((16, width - P_DEV), f32)], axis=1)
    small = [row_zero(grad_gain), table[:8], table[8:]]
    write_blocks(grad_w[0], place[2], dot(normed_t[:, :count], grad_query[...]))
    for i in range(2):
        part = dot(normed_t[...], grad_pairs[:, i * width : (i + 1) * width])
        write_blocks(grad_w[i + 1], place[3 + i], part, small)


def unpack_kernel(experts, heads, place, *rest):
    halves, (grad_w, grad_mix, gain_one, gain_two, router, table) = rest[:8], rest[8:14]
    staged, small, sems = rest[14:]
    half, _, width = halves[0].shape
    rows = width // (2 * half)
    copies = []
    for i in range(4):
        mine = place[2 + i]
        for j in range(2 * half):
            block = halves[2 * i + j // half][j % half].astype(f32)
            at = pl.multiple_of((j ^ mine) * rows, rows)
            staged[i, pl.ds(at, rows), :] = block[:rows]
            if i >= 2:
                small[i - 2, j ^ mine] = block[rows:]
        into = grad_mix if i == 3 else grad_w.at[:, pl.ds(i * width, width)]
        copies.append(pltpu.make_async_copy(staged.at[i], into, sems.at[i]))
        copies[-1].start()
    gain_one[...] = small[0, 0, 0, :]
    gain_two[...] = small[1, 0, 0, :]
    for i in range(experts // 8):
        router[i * 8 : (i + 1) * 8, :] = small[1, 1 + i]
    lines = jnp.concatenate([small[0, 1], small[0, 2]], axis=0)
    table[...] = lines[:heads, :32]
    for copy in copies:
        copy.wait()


def finish_kernel(x, gain, grad_hidden, grad_prompt, grad_rest, grad_input):
    values = x[...].astype(f32)
    scale = norm_rows(values)
    grad = jnp.concatenate([grad_prompt[...], grad_rest[...]], axis=0)
    weighted = grad * gain[...]
    inner = jnp.mean(weighted * values, axis=-1, keepdims=True)
    grad_input[...] = grad_hidden[...] + scale * weighted - values * (scale**3 * inner)


def permute(value, axis, offset):
    size = lax.axis_size(axis)
    return lax.ppermute(value, axis, [(i, i ^ offset) for i in range(size)])


def bits_of(size):
    return [1 << b for b in range(size.bit_length() - 1)]


def spread_far(block):
    held = {0: block}
    for bit in bits_of(lax.axis_size("dp"))[:0:-1]:
        held.update({k ^ bit: permute(v, "dp", bit) for k, v in list(held.items())})
    return held


def spread_near(held):
    held = held | {k ^ 1: permute(v, "dp", 1) for k, v in held.items()}
    return [held[k] for k in sorted(held)]


def exchange(blocks):
    size = len(blocks)
    got = {0: blocks[0]}
    for k in [*range(size // 2, size), *range(1, size // 2)]:
        got[k] = permute(blocks[k], "expert", k)
    return [got[k] for k in range(size)]


def swap(blocks):
    return lax.all_to_all(blocks, "expert", split_axis=0, concat_axis=0, tiled=True)


def add(left, right):
    return left.astype(f32) + right.astype(f32)


def after(value, *first):
    return lax.optimization_barrier((value, *first))[0]


def fold(held):
    held = dict(zip(range(0, 2 * len(held), 2), held))
    for bit in bits_of(lax.axis_size("dp"))[1:]:
        for k in [k for k in held if not k & bit]:
            held[k] = add(held[k], permute(held.pop(k | bit).astype(bf16), "dp", bit))
    return held[0]


halving = {"c": ("dp", 1), "x": ("dp", 2), "y": ("expert", 1), "z": ("expert", 2)}
orders = ["cxyz", "cyzx", "czxy", "cxyz"]


def block_index(order):
    index = jnp.int32(0)
    for name in order:
        axis, bit = halving[name]
        index = index * 2 + (lax.axis_index(axis) & bit) // bit
    return index


def halve(blocks, order):
    for name in order:
        half = blocks.shape[0] // 2
        blocks = add(blocks[:half], permute(blocks[half:], *halving[name])).astype(bf16)
    return blocks


def widen(blocks, order):
    for name in order[:0:-1]:
        blocks = jnp.concatenate([blocks, permute(blocks, *halving[name])], axis=0)
    return [blocks, permute(blocks, *halving[order[0]])]


def other_steps():
    return [(axis, bit) for axis in ("dp", "expert") for bit in bits_of(lax.axis_size(axis))
            if (axis, bit) not in halving.values()]


def sum_blocks(parts, *first):
    parts = [halve(part, order) for part, order in zip(parts, orders)]
    whole = jnp.concatenate(parts, axis=1)
    for step in other_steps():
        whole = add(whole, permute(whole, *step)).astype(bf16)
    whole = after(whole, *first)
    halves = []
    at = 0
    for part, order in zip(parts, orders):
        halves += widen(whole[:, at : at + part.shape[1]], order)
        at += part.shape[1]
    return halves


def body(
    block_input,
    gain_attn,
    w_qkv,
    w_mix,
    rel_bias,
    gain_ffn,
    w_router,
    w_up,
    w_down,
    routes,
    fill_order,
    grad_output,
):
    count, width = block_input.shape
    heads = rel_bias.shape[1]
    dp_size = lax.axis_size("dp")
    experts = w_router.shape[1]
    cap = 9 * 2 * count // (8 * experts)
    rows = (cap + 16) // 16 * 16
    slots = experts * rows
    keys = (dp_size + 1) * P_DEV
    hidden_units = w_up.shape[2] * dp_size
    place = [lax.axis_index("expert"), lax.axis_index("dp"), *map(block_index, orders)]
    place = jnp.stack(place).astype(jnp.int32)
    gain_one, gain_two = gain_attn.reshape(1, width), gain_ffn.reshape(1, width)

    others = spread_far(block_input[:P_DEV])
    w_up, others = lax.optimization_barrier((w_up, others))
    others = spread_near(others)[1:]
    ups = spread_far(w_up[0])
    ups_near = permute(w_up[0], "dp", 1)
    downs = lax.all_gather(w_down[0], "dp", axis=0)

    pos_c, pos_r, tops = call(
        functools.partial(route_kernel, experts, cap, rows),
        [
            like((count, 2), jnp.int32),
            like((2, count), jnp.int32),
            like((experts, rows, width), bf16),
        ],
        [],
        [place, routes.T, fill_order, grad_output],
        2 * slots * count * width,
        limit=16,
    )
    tops = swap(tops)
    normed_low, projected, tiles = call(
        project_kernel,
        [
            like((count, width), bf16),
            like((count, 3 * width), bf16),
            like((heads, 4, P_DEV, P_DEV), f32),
        ],
        [],
        [block_input, gain_one, w_qkv, rel_bias],
        6 * count * width * width,
        smem=0,
        limit=16,
    )
    ups_near, others = lax.optimization_barrier((ups_near, others))
    hidden, attended, gates, chances, pairs, normed_others, *sent = call(
        functools.partial(attend_kernel, dp_size, heads, cap, rows, experts),
        [
            like((count, width), f32),
            like((count, width), f32),
            like((count, P_DEV), f32),
            like((heads, keys, count), bf16),
            like((keys, 2 * width), bf16),
            like(((dp_size - 1) * P_DEV, width), bf16),
        ]
        + [like((rows, width), bf16)] * experts,
        [pltpu.VMEM((2, keys, count), f32)],
        [place, block_input, projected, gain_one, w_qkv, tiles, w_mix, gain_two, w_router, routes]
        + [pos_c, pos_r, *others],
        4 * keys * width * width + 4 * count * keys * width * 2,
        limit=28,
    )
    got = exchange(sent)
    ups_far = {k: v for k, v in ups.items() if k}
    ups_far, got[1] = lax.optimization_barrier((ups_far, got[1]))
    ups = {0: ups[0], 1: ups_near} | ups_far | {k ^ 1: permute(v, "dp", 1) for k, v in ups_far.items()}
    ups = [ups[k] for k in range(dp_size)]
    results = call(
        functools.partial(expert_kernel, experts, cap, rows),
        [like((rows, width), bf16)] * (2 * experts)
        + [like((slots, width), bf16)] * 2
        + [like((slots, hidden_units), bf16)] * 2,
        [],
        [place, tops, downs, *ups, *got],
        8 * slots * width * hidden_units,
        limit=34,
    )
    arrived, grad_out, active, grad_pre = results[2 * experts :]
    backs = exchange(results[experts : 2 * experts])
    returned = exchange(after(results[:experts], *backs))
    units = w_up.shape[2]
    (grads,) = call(
        weight_kernel,
        [like((dp_size, 2, width, units), bf16)],
        [],
        [place, arrived, grad_out, active, grad_pre],
        4 * slots * width * hidden_units,
        limit=28,
    )
    grads, backs = lax.optimization_barrier((grads, backs))
    grads = lax.psum_scatter(grads, "dp", scatter_dimension=0)
    grad_weights = [grads[i : i + 1].astype(f32) for i in range(2)]

    blocks = 1 << len(orders[0])
    part = like((blocks, width // blocks, width), bf16)
    more = like((blocks, width // blocks + 8, width), bf16)
    grad_hidden, grad_att, delta, mix = call(
        functools.partial(router_kernel, heads, cap, rows, experts),
        [
            like((count, width), f32),
            like((count, width), bf16),
            like((heads, count), f32),
            more,
        ],
        [pltpu.VMEM((slots, width), bf16)],
        [place, hidden, gates, pos_c, routes, gain_two, w_router, grad_output, attended, w_mix]
        + backs,
        4 * count * width * width + 2 * slots * count * width,
        limit=16,
    )
    results = call(
        functools.partial(backward_kernel, dp_size, heads),
        [part] * 2
        + [more, like((CLEN, width), f32)]
        + [like((dp_size // 2, P_DEV, width), bf16), like((P_DEV, width), f32)]
        + [like((P_DEV, width), bf16)] * (dp_size // 2 - 1),
        [
            pltpu.VMEM((4, P_DEV, P_DEV), f32),
            pltpu.VMEM((count, width), bf16),
            pltpu.VMEM((keys, 2 * width), bf16),
            pltpu.VMEM((width, keys), bf16),
            pltpu.VMEM((keys, width), bf16),
            pltpu.VMEM((16, 3 * P_DEV), f32),
        ],
        [place, grad_att, delta, chances, pairs, projected, normed_low, normed_others]
        + [gain_one, w_qkv],
        8 * keys * width * width + 4 * count * keys * width * 4,
        limit=28,
    )
    parts, (grad_rest, odd), even = results[:3], results[3:5], results[5:]
    parts, mix, returned = lax.optimization_barrier((parts, mix, returned))
    odd = permute(odd, "dp", 1)
    grad_prompt = fold([add(v, odd[i]) for i, v in enumerate(even)])
    (output,) = call(
        functools.partial(combine_kernel, experts, rows),
        [like((count, width), bf16)],
        [pltpu.VMEM((slots, width), bf16)],
        [hidden, gates, pos_c, *returned],
        4 * slots * count * width,
        smem=0,
        limit=12,
    )
    (grad_input,) = call(
        finish_kernel,
        [like((count, width), f32)],
        [],
        [block_input, gain_one, grad_hidden, grad_prompt, grad_rest],
        10 * count * width,
        smem=0,
        limit=8,
    )
    halves = sum_blocks([*parts, mix], output, grad_input)
    *halves, grad_up, grad_down = lax.optimization_barrier((*halves, *grad_weights))
    hbm = pl.BlockSpec(memory_space=pl.ANY)
    args = [place, *halves]
    grad_w, grad_mix, grad_one, grad_two, grad_router, grad_table = pl.pallas_call(
        functools.partial(unpack_kernel, experts, heads),
        out_shape=[
            like((width, 3 * width), f32),
            like((width, width), f32),
            like((width,), f32),
            like((width,), f32),
            like((experts, width), f32),
            like((heads, 32), f32),
        ],
        in_specs=[SMEM] + [VMEM] * (len(args) - 1),
        out_specs=[hbm] * 2 + [VMEM] * 4,
        scratch_shapes=[
            pltpu.VMEM((4, width, width), f32),
            pltpu.VMEM((2, blocks, 8, width), f32),
            pltpu.SemaphoreType.DMA((4,)),
        ],
        compiler_params=pltpu.CompilerParams(vmem_limit_bytes=24 * 1024 * 1024),
    )(*args)
    return (
        output,
        grad_input,
        grad_one,
        grad_w,
        grad_mix,
        grad_table.T,
        grad_two,
        grad_router.T,
        grad_up,
        grad_down,
    )


def solution(mesh):
    in_specs = (
        P(("dp", "expert"), None),
        P(),
        P(),
        P(),
        P(),
        P(),
        P(),
        P("expert", None, "dp"),
        P("expert", None, "dp"),
        P(("dp", "expert"), None),
        P(("dp", "expert"), None),
        P(("dp", "expert"), None),
    )
    out_specs = (
        P(("dp", "expert"), None),
        P(("dp", "expert"), None),
        P(),
        P(),
        P(),
        P(),
        P(),
        P(),
        P("expert", None, "dp"),
        P("expert", None, "dp"),
    )
    return jax.shard_map(body, mesh=mesh, in_specs=in_specs, out_specs=out_specs, check_vma=False)
```

```python
import functools
import math

import jax
import jax.numpy as jnp
from jax import lax
from jax.experimental import pallas as pl
from jax.experimental.pallas import tpu as pltpu
from jax.sharding import PartitionSpec as P

CLEN = 128
P_DEV = 128

epsilon = 1e-06
masked_score = -1e30
bucket_edges = [int(math.ceil(16 * 8 ** (step / 16))) for step in range(1, 16)]
bf16 = jnp.bfloat16
f32 = jnp.float32


def contract(left, right, left_dim, right_dim):
    dims = (((left_dim,), (right_dim,)), ((), ()))
    return lax.dot_general(left, right, dims, preferred_element_type=f32)


def dot(left, right):
    return contract(left, right, 1, 0)


def dot_cols(left, right):
    return contract(left, right, 1, 1)


def dot_rows(left, right):
    return contract(left, right, 0, 0)


def iota(shape, axis):
    return lax.broadcasted_iota(jnp.int32, shape, axis)


def like(shape, dtype):
    return jax.ShapeDtypeStruct(shape, dtype)


class Load:
    def __init__(self, source, into, sem):
        self.into = into
        self.copy = pltpu.make_async_copy(source, into, sem)
        self.started = self.waited = False

    def start(self):
        if not self.started:
            self.copy.start()
            self.started = True

    def __call__(self):
        self.start()
        if not self.waited:
            self.copy.wait()
            self.waited = True
        return self.into


class Near:
    def __init__(self, ref):
        self.into = ref

    def __call__(self):
        ref = self.into
        return ref[...].reshape(1, ref.shape[0]) if len(ref.shape) == 1 else ref


def start(*loads):
    for load in loads:
        if isinstance(load, Load):
            load.start()


class Store:
    def __init__(self, ref, into, sems):
        self.ref, self.into, self.sems = ref, into, sems
        self.copies = []

    def send(self, *pieces):
        if not pieces:
            copies = [pltpu.make_async_copy(self.ref, self.into, self.sems.at[0])]
        else:
            copies = [
                pltpu.make_async_copy(self.ref.at[i], self.into.at[i], self.sems.at[at])
                for at, i in enumerate(pieces, len(self.copies))
            ]
        for copy in copies:
            copy.start()
        self.copies += copies

    def begin(self, piece):
        pltpu.make_async_copy(self.ref.at[piece], self.into.at[piece], self.sems.at[piece]).start()

    def begun(self):
        self.copies += [
            pltpu.make_async_copy(self.ref.at[i], self.into.at[i], self.sems.at[i])
            for i in range(self.ref.shape[0])
        ]

    def send_part(self, index, *part):
        source, into = self.ref.at[part], self.into.at[part]
        self.copies.append(pltpu.make_async_copy(source, into, self.sems.at[index]))
        self.copies[-1].start()


def call(body, outs, scratch, args, flops, raw=0, raw_outs=0, near=0):
    args, outs = list(args), list(outs)
    count, results = len(args), len(outs)
    flat = [a.ndim == 1 or i < near for i, a in enumerate(args)]
    moved = [i for i in range(count - raw) if not flat[i]]
    direct = [len(o.shape) == 1 or i >= results - raw_outs for i, o in enumerate(outs)]
    pieces = 32

    def kernel(*refs):
        given, refs = refs[:count], refs[count:]
        made, refs = refs[:results], refs[results:]
        held, refs = refs[: len(moved)], refs[len(moved) :]
        ready, refs = refs[: results - sum(direct)], refs[results - sum(direct) :]
        in_sems, out_sems, *rest = refs
        loads = []
        for i in range(count):
            if i in moved:
                at = moved.index(i)
                loads.append(Load(given[i], held[at], in_sems.at[at]))
            elif flat[i]:
                loads.append(Near(given[i]))
            else:
                loads.append(given[i])
        ready = iter(ready)
        stores = [
            made[i] if direct[i] else Store(next(ready), made[i], out_sems.at[i])
            for i in range(results)
        ]
        body(loads, stores, *rest)
        for load in loads:
            if isinstance(load, Load):
                load()
        stores = [store for store in stores if isinstance(store, Store)]
        for store in stores:
            if not store.copies:
                store.send()
        for store in stores:
            for copy in store.copies:
                copy.wait()

    held = [args[i] for i in moved] + [o for o, is_direct in zip(outs, direct) if not is_direct]
    sems = pltpu.SemaphoreType.DMA
    size = sum(math.prod(a.shape) * a.dtype.itemsize for a in args + outs)
    room = [pltpu.VMEM(a.shape, a.dtype) for a in held]
    made = pl.pallas_call(
        kernel,
        out_shape=outs,
        in_specs=[pl.BlockSpec(memory_space=pltpu.VMEM if f else pl.ANY) for f in flat],
        out_specs=[
            pl.BlockSpec(memory_space=pltpu.VMEM if len(o.shape) == 1 else pl.ANY) for o in outs
        ],
        scratch_shapes=room + [sems((max(len(moved), 1),)), sems((results, pieces))] + scratch,
        compiler_params=pltpu.CompilerParams(vmem_limit_bytes=58 << 20),
        cost_estimate=pl.CostEstimate(flops=flops, bytes_accessed=size, transcendentals=0),
    )(*args)
    return list(made)


def bucket_of(distance):
    beyond = sum(((distance >= edge).astype(jnp.int32) for edge in bucket_edges))
    return jnp.clip(jnp.where(distance < 16, distance, 16 + beyond), 0, 31)


def thirds(value):
    high = value.astype(bf16).astype(f32)
    mid = (value - high).astype(bf16).astype(f32)
    return high, mid, value - high - mid


def pieces_of(value, count=3):
    return [v.astype(bf16) for v in thirds(value)[:count]]


def norm_rows(values):
    return lax.rsqrt(jnp.mean(values * values, axis=-1, keepdims=True) + epsilon)


def columns_of(lines):
    count = lines[0].shape[1]
    lines = [line.astype(f32) for line in lines]
    lines += [jnp.zeros((8 - len(lines), count), f32)]
    columns = jnp.transpose(jnp.concatenate(lines, axis=0))
    return [columns[:, c : c + 1] for c in range(len(lines) - 1)]


def route_kernel(experts, cap, rows, loads, stores):
    routes, fill_order, grad_out = loads
    pos, sent = stores
    start(*loads)
    routes = routes()[...]
    count = routes.shape[1]
    order = jnp.broadcast_to(fill_order()[...], (16, 2 * count))
    coarse = order & ~31
    order = jnp.where(iota(order.shape, 0) < 8, coarse, order - coarse).astype(f32).astype(bf16)
    at, to = iota((2 * count, 2 * count), 0), iota((2 * count, 2 * count), 1)
    pick = (at == jnp.where(to < count, 2 * to, 2 * (to - count) + 1)).astype(f32).astype(bf16)
    order = dot(order, pick)
    order = order[:8] + order[8:]
    orow = [order[:1, :count], order[:1, count:]]
    row = [routes[c : c + 1, :].astype(f32) for c in range(2)]
    col = columns_of([*row, *orow])
    col, ocol = col[:2], col[2:]
    slots = []
    for c in range(2):
        rank = jnp.zeros((1, count), f32)
        for other in range(2):
            hit = (col[other] == row[c]) & (ocol[other] < orow[c])
            rank += jnp.sum(hit.astype(f32), axis=0, keepdims=True)
        rank = rank.astype(jnp.int32)
        slot = routes[c : c + 1, :] * rows + rank
        slots.append(jnp.where(rank < cap, slot, -1))
    pos.ref[...] = jnp.concatenate([*slots, jnp.zeros((6, count), jnp.int32)], axis=0)
    pos.send()
    grad_top = grad_out()[...]
    for k in range(experts):
        index = iota((rows, count), 0) + k * rows
        onehot = ((index == slots[0]) | (index == slots[1])).astype(f32).astype(bf16)
        at = slice(k * rows, (k + 1) * rows)
        sent.ref[at, :] = dot(onehot, grad_top).astype(bf16)
        sent.send_part(k, at)


def bias_tiles(table, tiles):
    heads, buckets = table.shape
    width = 2 * P_DEV
    onehot = (bucket_of(iota((buckets, width), 1)) == iota((buckets, width), 0)).astype(f32)
    line = sum(dot(part, onehot.astype(bf16)) for part in pieces_of(table))
    causal = iota((P_DEV, P_DEV), 1) >= iota((P_DEV, P_DEV), 0)
    for h in range(heads):
        spread = jnp.broadcast_to(line[h : h + 1, :], (P_DEV, width))
        rolled = pltpu.roll(spread, 0, 1, stride=1, stride_axis=0)
        tiles[h, 0] = jnp.full((P_DEV, P_DEV), masked_score, f32)
        tiles[h, 1] = jnp.where(causal, rolled[:, :P_DEV], masked_score)
        tiles[h, 2] = rolled[:, P_DEV:]
        tiles[h, 3] = jnp.broadcast_to(line[h : h + 1, width - 1 : width], (P_DEV, P_DEV))


def tile_index(block, dp_size, dp_index, continuation):
    if block == 0:
        return 1 if continuation else 0
    key = dp_index ^ (block - 1)
    if continuation:
        return jnp.minimum(dp_size - key, 2) + 1
    if block == 1:
        return 1
    return jnp.clip(dp_index - key, -1, 2) + 1


def attend_kernel(dp_size, heads, cap, rows, experts, loads, stores, tiles, scores):
    x, *others, w_qkv, gain, table, w_mix, gain_ffn, router, routes, pos = loads
    hidden, kept, gates, chances, pairs, query_rows, normed_all, sent = stores
    start(x, table, *others, w_qkv)
    count, width = x.into.shape
    head_size = width // heads
    dp_index = lax.axis_index("dp")
    values = x()[...].astype(f32)
    low = values * norm_rows(values) * gain()
    normed_all.ref[0:CLEN, :] = low[P_DEV:].astype(bf16)
    normed_all.ref[CLEN:count, :] = low[:P_DEV].astype(bf16)
    for k, other in enumerate(others):
        values = other()[...].astype(f32)
        at = slice((k + 2) * P_DEV, (k + 3) * P_DEV)
        normed_all.ref[at, :] = (values * norm_rows(values) * gain()).astype(bf16)
    normed_all.send()
    bias_tiles(table()[...], tiles)
    pairs, queries, chance = pairs, query_rows.ref, chances.ref
    weights = w_qkv()
    start(w_mix, router, routes, pos)
    queries[...] = dot(normed_all.ref[:count, :], weights[:, :width]).astype(bf16)
    query_rows.send()
    pairs.ref[...] = dot(normed_all.ref[...], weights[:, width:]).astype(bf16)
    pairs.send()
    left = iota((count, P_DEV), 1) < head_size
    for p in range(heads // 2):
        cut = slice(p * P_DEV, (p + 1) * P_DEV)
        key = pairs.ref[:, cut]
        value_t = jnp.transpose(pairs.ref[:, width + p * P_DEV : width + (p + 1) * P_DEV])
        query = queries[:, cut] * bf16(head_size**-0.5)
        zero = jnp.zeros_like(query)
        parts = []
        for s in range(2):
            h = 2 * p + s
            part = jnp.where(left, query, zero) if s == 0 else jnp.where(left, zero, query)
            raw = dot_cols(key, part)
            top = None
            for b in range(dp_size + 1):
                bias = jnp.concatenate(
                    [
                        tiles[h, tile_index(b, dp_size, dp_index, True)],
                        tiles[h, tile_index(b, dp_size, dp_index, False)],
                    ],
                    axis=1,
                )
                block = raw[b * P_DEV : (b + 1) * P_DEV, :] + bias
                scores[s, b * P_DEV : (b + 1) * P_DEV, :] = block
                most = jnp.max(block, axis=0, keepdims=True)
                top = most if top is None else jnp.maximum(top, most)
            total = jnp.zeros((1, count), f32)
            for b in range(dp_size + 1):
                weight = jnp.exp(scores[s, b * P_DEV : (b + 1) * P_DEV, :] - top)
                scores[s, b * P_DEV : (b + 1) * P_DEV, :] = weight
                total += jnp.sum(weight, axis=0, keepdims=True)
            inverse = 1.0 / total
            chance[h, :, :] = (scores[s] * inverse).astype(bf16)
            parts.append(dot(value_t[s * head_size : (s + 1) * head_size, :], chance[h]))
        part = jnp.transpose(jnp.concatenate(parts, axis=0))
        kept.ref[P_DEV:, cut] = part[:CLEN]
        kept.ref[:P_DEV, cut] = part[CLEN:]
        chances.send(2 * p, 2 * p + 1)
    kept.send()
    hid = x()[...].astype(f32) + dot(kept.ref[...].astype(bf16), w_mix()[...])
    hidden.ref[...] = hid
    hidden.send()
    normed_two = hid * norm_rows(hid) * gain_ffn()
    weights = jnp.concatenate([v.astype(f32) for v in pieces_of(router()[...])], axis=0).astype(bf16)
    logits = sum(dot_cols(weights, part) for part in pieces_of(normed_two, 2))
    logits = logits[:experts] + logits[experts : 2 * experts] + logits[2 * experts :]
    row = iota(logits.shape, 0)
    routes = routes()[...]
    pick = [
        jnp.sum(jnp.where(row == routes[c : c + 1, :], logits, 0.0), axis=0, keepdims=True)
        for c in range(2)
    ]
    most = jnp.maximum(pick[0], pick[1])
    raised = [jnp.exp(v - most) for v in pick]
    gate = [v / (raised[0] + raised[1]) for v in raised]
    gates.ref[...] = jnp.concatenate([*gate, jnp.zeros((6, count), f32)], axis=0)
    gates.send()
    pos = pos()[...]
    pos_col = columns_of([pos[c : c + 1, :] for c in range(2)])
    pos_col = [v.astype(jnp.int32) for v in pos_col]
    gate = columns_of(gate)
    lane = iota((count, P_DEV), 1)
    low = normed_two.astype(bf16)
    for k in range(experts):
        index = iota((rows, count), 0) + k * rows
        onehot = (index == pos[0:1, :]) | (index == pos[1:2, :])
        block = dot(onehot.astype(f32).astype(bf16), low)
        line = jnp.zeros((1, P_DEV), f32)
        for c in range(2):
            mine = pos_col[c] == lane + k * rows
            line += jnp.sum(jnp.where(mine, gate[c], 0.0), axis=0, keepdims=True)
        line = jnp.concatenate([*thirds(line), jnp.zeros((1, width - 3 * P_DEV), f32)], axis=1)
        at = slice(k * rows, (k + 1) * rows)
        sent.ref[at, :] = jnp.where(iota((rows, width), 0) == cap, line, block).astype(bf16)
        sent.send_part(k, at)


def gelu_parts(value):
    factor = math.sqrt(2 / math.pi)
    square = value * value
    bend = jnp.tanh(factor * value * (1.0 + 0.044715 * square))
    half = 0.5 * (1.0 + bend)
    slope = half + (0.5 * factor) * value * (1.0 - bend * bend) * (1.0 + 0.134145 * square)
    return value * half, slope


def gather_columns(blocks, into, sems):
    width = into.shape[1] // len(blocks)
    return [
        Load(block, into.at[:, i * width : (i + 1) * width], sems.at[i])
        for i, block in enumerate(blocks)
    ]


def early_kernel(loads, stores, down, early, sems):
    tops, downs = loads
    dp_index = lax.axis_index("dp")
    blocks, width, units = downs.shape
    copies = gather_columns([downs.at[q ^ dp_index] for q in range(blocks)], down, sems.at[0])
    sent = []
    start(tops, *copies[:2])
    for q in range(blocks):
        at = slice(q * units, (q + 1) * units)
        copies[q]()
        start(*copies[q + 1 : q + 3])
        early[q] = dot(tops()[...], down[:, at]).astype(bf16)
        sent.append(pltpu.make_async_copy(early.at[q], stores[0].at[q], sems.at[1, q]))
        sent[-1].start()
    for copy in sent:
        copy.wait()


def payload_line(block, cap, index):
    rows = block.shape[0]
    line = block[rows - 16 :, index * P_DEV : (index + 1) * P_DEV].astype(f32)
    return line[cap - rows + 16 : cap - rows + 17, :]


def gate_column(block, cap):
    line = sum(payload_line(block, cap, i) for i in range(3))
    same = iota((block.shape[0], P_DEV), 0) == iota((block.shape[0], P_DEV), 1)
    return jnp.sum(jnp.where(same, line, 0.0), axis=1, keepdims=True)


def expert_kernel(cap, rows, blocks, loads, stores, up, early, total, product, active, grad_pre, sems):
    got = loads[0]
    back, *kept = stores
    slots, width = got.into.shape
    units = up.shape[1] // blocks
    start(got)
    for q in range(blocks):
        pltpu.make_async_copy(loads[1+q], up.at[:, q*units:(q+1)*units], sems.at[0,q]).start()
        pltpu.make_async_copy(loads[-1].at[q], early.at[q], sems.at[1,q]).start()
    pieces = [slice(at, at + rows) for at in range(0, slots, rows)]
    same = iota((rows, P_DEV), 0) == iota((rows, P_DEV), 1)
    gates = [gate_column(got()[at, :], cap) for at in pieces]
    chunk = product.shape[2]
    total[...] = jnp.zeros_like(total)
    def step(q, carry):
        base = pl.multiple_of(q*units, units)
        pltpu.make_async_copy(loads[1], up.at[:, pl.ds(base, units)], sems.at[0,q]).wait()
        pltpu.make_async_copy(loads[-1].at[q], early.at[q], sems.at[1,q]).wait()
        for i in range(units//chunk):
            to = pl.ds(pl.multiple_of(base + i*chunk, chunk), chunk)
            product[i % 2] = dot(got()[...], up[:, to])
            for at, gate in zip(pieces, gates):
                low, slope = gelu_parts(product[i % 2, at, :])
                active[at, to] = low.astype(bf16)
                grad = early[q, at, i * chunk : (i + 1) * chunk].astype(f32)
                both = grad * low
                total[at, :] += sum(both[:, j : j + P_DEV] for j in range(0, chunk, P_DEV))
                grad_pre[at, to] = (grad * slope * gate).astype(bf16)
        for i, part in enumerate((active, grad_pre)):
            pltpu.make_async_copy(part.at[:, pl.ds(base, units)], kept[i].at[q], sems.at[2 + i, q]).start()
        return carry
    lax.fori_loop(0, blocks, step, 0)
    half = len(pieces) // 2 * rows
    value = [dot_cols(grad_pre[i : i + half, :], up[...]) for i in (0, half)]
    for k, at in enumerate(pieces):
        line = jnp.sum(total[at, :], axis=1, keepdims=True)
        line = jnp.sum(jnp.where(same, line, 0.0), axis=0, keepdims=True)
        line = [*thirds(line), jnp.zeros((1, width - 3 * P_DEV), f32)]
        line = jnp.concatenate(line, axis=1)
        part = value[at.start // half][at.start % half :][:rows]
        back.ref[at, :] = jnp.where(iota((rows, width), 0) == cap, line, part).astype(bf16)
        back.send_part(k, at)
    for q in range(blocks):
        for i, part in enumerate((active, grad_pre)):
            pltpu.make_async_copy(part.at[:, q*units:(q+1)*units], kept[i].at[q], sems.at[2 + i, q]).wait()

def weight_kernel(cap, rows, blocks, loads, stores, grad_pre, active, down, sems):
    got, tops, *whole, downs = loads
    dp_index = lax.axis_index("dp")
    start(got, tops)
    units = active.shape[1] // blocks

    def copies_of(q):
        cut = pl.ds(pl.multiple_of(q * units, units), units)
        sources = (whole[0].at[q], whole[1].at[q], downs.at[q ^ dp_index])
        return [
            pltpu.make_async_copy(source, into.at[:, cut], sems.at[i, q])
            for i, (source, into) in enumerate(zip(sources, (grad_pre, active, down)))
        ]

    for q in range(blocks):
        for copy in copies_of(q):
            copy.start()
    grads, result = stores
    grad_out = []
    for at in range(0, got.into.shape[0], rows):
        gate = gate_column(got()[at : at + rows, :], cap)
        grad_out.append((gate * tops()[at : at + rows, :].astype(f32)).astype(bf16))
    rows_t = jnp.transpose(got()[...])
    grad_t = jnp.transpose(jnp.concatenate(grad_out, axis=0))

    def step(q, carry):
        for copy in copies_of(q):
            copy.wait()
        cut = pl.ds(pl.multiple_of(q * units, units), units)
        grads.ref[q ^ dp_index, 0] = dot(rows_t, grad_pre[:, cut]).astype(bf16)
        grads.ref[q ^ dp_index, 1] = dot(grad_t, active[:, cut]).astype(bf16)
        grads.begin(q ^ dp_index)
        return carry

    lax.fori_loop(0, blocks, step, 0)
    grads.begun()
    result.ref[...] = dot_cols(active[...], down[...]).astype(bf16)


def combine_kernel(loads, stores):
    hidden, gates, pos, back = loads
    (output,) = stores
    start(*loads)
    columns = columns_of([gates()[0:1, :], gates()[1:2, :], pos()[0:1, :], pos()[1:2, :]])
    held = back()[...]
    index = iota((hidden.into.shape[0], held.shape[0]), 1)
    total = hidden()[...]
    for c in range(2):
        onehot = (index == columns[2 + c].astype(jnp.int32)).astype(f32).astype(bf16)
        total += columns[c] * dot(onehot, held)
    output.ref[...] = total.astype(bf16)


def diagonal_sums(values):
    size, width = values.shape
    while size > 8:
        size //= 2
        values = values[:size] + pltpu.roll(values[size:], width - size, 1)
    row = iota(values.shape, 0)
    for bit in (4, 2, 1):
        values = jnp.where((row & bit) != 0, pltpu.roll(values, width - bit, 1), values)
    return jnp.sum(values, axis=0, keepdims=True)


def backward_kernel(dp_size, heads, cap, loads, stores, grad_att, delta, sums, grad_query,
                    grad_pairs, normed_t, lines, staged, sems):
    back, hidden, gates, pos, routes, gain_ffn, router, grad_output, kept, w_mix = loads[:10]
    query_rows, pairs, chances, normed_all, gain, w_qkv = loads[10:]
    start(back, gates, pos, routes, hidden, router, grad_output, kept, w_mix)
    experts = router.into.shape[0]
    rows = back.into.shape[0] // experts
    (grad_hidden, grad_rest, grad_odd), stores = stores[:3], stores[3:]
    parts = staged.shape[0]
    grad_even, halves = stores[: -2 * parts], stores[-2 * parts :]
    mine = [block_index(order) for order in orders]
    width = hidden.into.shape[1]
    blocks, step_rows, part_width = staged.shape[1], width // staged.shape[1], staged.shape[3]
    copies = []

    def put(first, value):
        for at in range(0, value.shape[1], 256):
            index, into = divmod(first + at, part_width)
            for p in range(blocks):
                part = value[p * step_rows : (p + 1) * step_rows, at : at + 256]
                to = slice(into, into + 256)
                staged[index, p ^ mine[index], 0:step_rows, to] = part.astype(bf16)

    def send(index, small=()):
        half = blocks // 2
        count = step_rows + (8 if small else 0)
        for p in range(blocks if small else 0):
            more = small[p] if p < len(small) else jnp.zeros((8, width), f32)
            staged[index, p ^ mine[index], step_rows:, 0:width] = more.astype(bf16)
        for i in range(2):
            source = staged.at[index, i * half : (i + 1) * half, 0:count]
            into = halves[2 * index + i]
            copies.append(pltpu.make_async_copy(source, into, sems.at[index, i]))
            copies[-1].start()

    count, width = hidden.into.shape
    head_size = width // heads
    given = [gates()[0:1, :], gates()[1:2, :]]
    given += [ref[c : c + 1, :] for ref in (pos(), routes()) for c in range(2)]
    columns = columns_of(given)
    gate = columns[:2]
    pos, routes = ([v.astype(jnp.int32) for v in columns[i : i + 2]] for i in (2, 4))
    index = iota((count, experts * rows), 1)
    onehot = (index == pos[0]) | (index == pos[1])
    grad_two = dot(onehot.astype(f32).astype(bf16), back()[...])
    lane = iota((count, P_DEV), 1)
    found = [jnp.zeros((count, P_DEV), f32) for c in range(2)]
    for k in range(experts):
        line = sum(payload_line(back()[k * rows : (k + 1) * rows, :], cap, i) for i in range(3))
        for c in range(2):
            found[c] += jnp.where(pos[c] == lane + k * rows, line, 0.0)
    grad_gate = [jnp.sum(v, axis=1, keepdims=True) for v in found]
    hid = hidden()[...]
    start(query_rows, pairs, chances)
    scale = norm_rows(hid)
    normed_two = hid * scale * gain_ffn()
    slope = gate[0] * gate[1] * (grad_gate[0] - grad_gate[1])
    lane = iota((count, experts), 1)
    grad_logits = jnp.where(lane == routes[0], slope, 0.0) - jnp.where(lane == routes[1], slope, 0.0)
    left = thirds(grad_logits)
    right = thirds(router()[...])
    pairs_of = [(0, 0), (0, 1), (1, 0), (0, 2), (1, 1), (2, 0)]
    left_all = jnp.concatenate([left[i] for i, _ in pairs_of], axis=1).astype(bf16)
    right_all = jnp.concatenate([right[i] for _, i in pairs_of], axis=0).astype(bf16)
    grad_two += dot(left_all, right_all)
    left = jnp.transpose(jnp.concatenate(left, axis=1)).astype(bf16)
    grad_router = sum(dot(left, part) for part in pieces_of(normed_two, 2))
    grad_router = grad_router[:experts] + grad_router[experts : 2 * experts] + grad_router[2 * experts :]
    grad_gain_ffn = jnp.sum(grad_two * hid * scale, axis=0, keepdims=True)
    weighted = grad_two * gain_ffn()
    inner = jnp.mean(weighted * hid, axis=-1, keepdims=True)
    grad_hid = grad_output()[...].astype(f32) + scale * weighted - hid * (scale**3 * inner)
    grad_hidden.ref[...] = grad_hid
    grad_hidden.send()
    mixed = grad_hid.astype(bf16)
    att = kept()[...]
    weights = w_mix()[...]
    start(normed_all, w_qkv)
    top = dot_cols(mixed, weights).astype(bf16)
    grad_att[0:CLEN, :] = top[P_DEV:]
    grad_att[CLEN:, :] = top[:P_DEV]
    put(3 * width, dot_rows(att.astype(bf16), mixed))
    prod_t = jnp.transpose(top.astype(f32) * att)
    for h in range(heads):
        line = prod_t[h * head_size : (h + 1) * head_size, :]
        line = jnp.sum(line, axis=0, keepdims=True)
        delta[h : h + 1, :] = jnp.concatenate([line[:, P_DEV:], line[:, :P_DEV]], axis=1)
    dp_index = lax.axis_index("dp")
    left = iota((count, P_DEV), 1) < head_size
    left_keys = iota((pairs.into.shape[0], P_DEV), 1) < head_size
    lines[...] = jnp.zeros_like(lines)
    queries, pairs_ref, chances = query_rows(), pairs(), chances()
    for p in range(heads // 2):
        cut = slice(p * P_DEV, (p + 1) * P_DEV)
        cut_value = slice(width + p * P_DEV, width + (p + 1) * P_DEV)
        key_t = jnp.transpose(pairs_ref[:, cut])
        value = pairs_ref[:, cut_value]
        query = queries[:, cut] * bf16(head_size**-0.5)
        top = grad_att[:, cut]
        zero = jnp.zeros_like(top)
        grad_q, grad_k, grad_v = [], [], []
        for s in range(2):
            h = 2 * p + s
            part = jnp.where(left, top, zero) if s == 0 else jnp.where(left, zero, top)
            grad_chance = dot_cols(value, part)
            chance = chances[h]
            grad_score = (chance.astype(f32) * (grad_chance - delta[h : h + 1, :])).astype(bf16)
            grad_v.append(dot(chance, top))
            grad_k.append(dot(grad_score, query))
            grad_q.append(dot(key_t[s * head_size : (s + 1) * head_size, :], grad_score))
            sums[...] = jnp.zeros_like(sums)
            for b in range(dp_size + 1):
                tile = grad_score[b * P_DEV : (b + 1) * P_DEV, :].astype(f32)
                sums[tile_index(b, dp_size, dp_index, True)] += tile[:, :P_DEV]
                if b > 0:
                    sums[tile_index(b, dp_size, dp_index, False)] += tile[:, P_DEV:]
            both = jnp.concatenate([sums[1], sums[2]], axis=1)
            lines[h : h + 1, : 2 * P_DEV] = diagonal_sums(both)
            lines[h : h + 1, 2 * P_DEV :] = jnp.sum(sums[3], axis=0, keepdims=True)
        grad_pairs[:, cut] = jnp.where(left_keys, grad_k[0], grad_k[1]).astype(bf16)
        grad_pairs[:, cut_value] = jnp.where(left_keys, grad_v[0], grad_v[1]).astype(bf16)
        grad_q = jnp.transpose(jnp.concatenate(grad_q, axis=0) * head_size**-0.5)
        grad_query[:, cut] = grad_q.astype(bf16)
    normed_all = normed_all()
    normed_t[...] = jnp.transpose(normed_all[...])
    w_qkv = w_qkv()
    grad_low = dot_cols(grad_pairs[...], w_qkv[:, width:])
    for k in range(1, dp_size):
        part = grad_low[(k + 1) * P_DEV : (k + 2) * P_DEV].astype(bf16)
        if k % 2:
            grad_odd.ref[k // 2] = part
        else:
            grad_even[k // 2].ref[...] = part
            grad_even[k // 2].send()
    grad_odd.send()
    own = grad_low[:count] + dot_cols(grad_query[...], w_qkv[:, :width])
    grad_rest.ref[...] = own[:CLEN]
    grad_rest.send()
    grad_even[0].ref[...] = own[CLEN:]
    grad_even[0].send()
    grad_gain = jnp.sum(own * normed_all[:count, :].astype(f32), axis=0, keepdims=True)
    grad_gain += jnp.sum(
        grad_low[count:] * normed_all[count:, :].astype(f32), axis=0, keepdims=True
    )
    grad_gain = grad_gain / gain()
    distance = iota((lines.shape[1], P_DEV), 0)
    bucket = jnp.where(distance < 2 * P_DEV, bucket_of(distance), 31)
    onehot = (bucket == iota((lines.shape[1], P_DEV), 1)).astype(f32).astype(bf16)
    table = sum(dot(part, onehot) for part in pieces_of(lines[...]))
    table = jnp.concatenate([table, jnp.zeros((16, width - P_DEV), f32)], axis=1)
    row = iota((8, width), 0)
    small = [jnp.where(row == 0, grad_gain, jnp.where(row == 1, grad_gain_ffn, 0.0))]
    small += [table[:8], table[8:]]
    small += [grad_router[i : i + 8] for i in range(0, experts, 8)]
    put(0, dot(normed_t[:, :count], grad_query[...]))
    put(width, dot(normed_t[...], grad_pairs[:, :width]))
    send(0)
    put(2 * width, dot(normed_t[...], grad_pairs[:, width:]))
    send(1)
    send(2, small)
    for copy in copies:
        copy.wait()


def unpack_kernel(experts, heads, loads, stores, held, staged, small, sems_in, sems):
    gain_one, gain_two, router, table, grad_w, grad_mix = stores
    half, _, part_width = loads[0].shape
    parts = len(loads) // 2
    width, rows = grad_mix.shape[1], staged.shape[0] // (2 * half)
    halves = []
    for index in range(parts):
        count = loads[2 * index].shape[1]
        for j in range(2):
            into = held.at[index, j * half : (j + 1) * half, 0:count]
            halves.append(Load(loads[2 * index + j], into, sems_in.at[index, j]))
    start(*halves)
    for load in halves:
        load()
    copies = []
    for p in range(2 * half):
        at = slice(p * rows, (p + 1) * rows)
        for index in range(parts):
            block = held[index, p ^ block_index(orders[index])].astype(f32)
            staged[at, index * part_width : (index + 1) * part_width] = block[:rows]
        small[p] = block[rows : rows + 8]
        for i, into in enumerate((grad_w, grad_mix)):
            cut = slice(0, 3 * width) if i == 0 else slice(3 * width, 4 * width)
            copies.append(pltpu.make_async_copy(staged.at[at, cut], into.at[at], sems.at[i, p]))
            copies[-1].start()
    gain_one[...] = small[0, 0, :width]
    gain_two[...] = small[0, 1, :width]
    lines = jnp.concatenate([small[1], small[2]], axis=0)
    table.ref[...] = lines[:heads, :32]
    for i in range(experts // 8):
        router.ref[i * 8 : (i + 1) * 8, :] = small[3 + i][:, :width]
    for copy in copies:
        copy.wait()


def finish_kernel(loads, stores):
    x, gain, grad_hidden, grad_prompt, grad_rest = loads
    start(*loads)
    values = x()[...].astype(f32)
    scale = norm_rows(values)
    grad = jnp.concatenate([grad_prompt()[...], grad_rest()[...]], axis=0)
    weighted = grad * gain()
    inner = jnp.mean(weighted * values, axis=-1, keepdims=True)
    stores[0].ref[...] = grad_hidden()[...] + scale * weighted - values * (scale**3 * inner)


def permute(value, axis, offset):
    size = lax.axis_size(axis)
    return lax.ppermute(value, axis, [(i, i ^ offset) for i in range(size)])


def bits_of(size):
    return [1 << b for b in range(size.bit_length() - 1)]


def spread_far(block):
    held = {0: block}
    for bit in bits_of(lax.axis_size("dp"))[:0:-1]:
        held.update({k ^ bit: permute(v, "dp", bit) for k, v in list(held.items())})
    return held


def spread_near(held):
    held = held | {k ^ 1: permute(v, "dp", 1) for k, v in held.items()}
    return [held[k] for k in sorted(held)]


def swap(blocks):
    return lax.all_to_all(blocks, "expert", split_axis=0, concat_axis=0, tiled=True)


def add(left, right):
    return left.astype(f32) + right.astype(f32)


def after(value, *first):
    return lax.optimization_barrier((value, *first))[0]


halving = {"c": ("dp", 1), "x": ("dp", 2), "y": ("expert", 1), "z": ("expert", 2)}
orders = ["cyzx", "czyx", "cyzx"]
widening = ["xzy", "xyz", "zyx"]


def block_index(order):
    index = jnp.int32(0)
    for name in order:
        axis, bit = halving[name]
        index = index * 2 + (lax.axis_index(axis) & bit) // bit
    return index


def halve(keep, send, order):
    for name in order[:-1]:
        blocks = add(keep, permute(send, *halving[name])).astype(bf16)
        half = blocks.shape[0] // 2
        keep, send = blocks[:half], blocks[half:]
    return add(keep, permute(send, *halving[order[-1]])).astype(bf16)


def widen(blocks, order, back):
    for name in back:
        more = permute(blocks, *halving[name])
        blocks = jnp.concatenate([blocks, more], axis=order.index(name))
    return blocks


def other_steps():
    return [(axis, bit) for axis in ("dp", "expert") for bit in bits_of(lax.axis_size(axis))
            if (axis, bit) not in halving.values()]


def sum_blocks(parts, first):
    parts = [halve(*part, order) for part, order in zip(parts, orders)]
    whole = jnp.concatenate(parts, axis=1)
    for step in other_steps():
        whole = add(whole, permute(whole, *step)).astype(bf16)
    wide = []
    at = 0
    for part, order, back in zip(parts, orders, widening):
        block = whole[:, at : at + part.shape[1]]
        block = block.reshape((1,) * len(order) + block.shape[1:])
        wide.append(widen(block, order, back[:-1]))
        at += part.shape[1]
    wide[-1], first = lax.optimization_barrier((wide[-1], first))
    halves = []
    for block, order, back in zip(wide, orders, widening):
        block = widen(block, order, back[-1:])
        block = block.reshape(-1, *block.shape[-2:])
        halves += [block, permute(block, *halving[order[0]])]
    return halves, first


def body(
    block_input,
    gain_attn,
    w_qkv,
    w_mix,
    rel_bias,
    gain_ffn,
    w_router,
    w_up,
    w_down,
    routes,
    fill_order,
    grad_output,
):
    count, width = block_input.shape
    heads = rel_bias.shape[1]
    dp_size = lax.axis_size("dp")
    experts = w_router.shape[1]
    cap = 9 * 2 * count // (8 * experts)
    rows = (cap + 16) // 16 * 16
    slots = experts * rows
    keys = (dp_size + 1) * P_DEV
    units = w_up.shape[2]
    hidden_units = units * dp_size
    routes, router = routes.T, w_router.T
    packed = like((slots, width), bf16)

    others = spread_far(block_input[:P_DEV])
    downs = lax.all_gather(w_down[0], "dp", axis=0)
    pos, tops = call(
        functools.partial(route_kernel, experts, cap, rows),
        [like((8, count), jnp.int32), packed],
        [],
        [routes, fill_order, grad_output],
        2 * slots * count * width,
    )
    tops, others = lax.optimization_barrier((tops, others))
    tops = swap(tops)
    others = spread_near(others)[1:]
    ups_near = permute(w_up[0], "dp", 1)
    ups_near, others = lax.optimization_barrier((ups_near, others))
    hidden, kept, gates, chances, pairs, query_rows, normed_all, sent = call(
        functools.partial(attend_kernel, dp_size, heads, cap, rows, experts),
        [
            like((count, width), f32),
            like((count, width), f32),
            like((8, count), f32),
            like((heads, keys, count), bf16),
            like((keys, 2 * width), bf16),
            like((count, width), bf16),
            like((keys, width), bf16),
            packed,
        ],
        [
            pltpu.VMEM((heads, 4, P_DEV, P_DEV), f32),
            pltpu.VMEM((2, keys, count), f32),
        ],
        [block_input, *others, w_qkv, gain_attn, rel_bias.T, w_mix, gain_ffn, router]
        + [routes, pos],
        4 * keys * width * width + 4 * count * keys * width * 2,
    )
    got = swap(sent)
    sems = pltpu.SemaphoreType.DMA
    (early,) = call(
        early_kernel,
        [like((dp_size, slots, units), bf16)],
        [
            pltpu.VMEM((width, hidden_units), bf16),
            pltpu.VMEM((dp_size, slots, units), bf16),
            sems((2, dp_size)),
        ],
        [tops, downs],
        2 * slots * width * hidden_units,
        raw=1,
        raw_outs=1,
    )
    ups = spread_far(after(w_up, sent)[0])
    del ups[0]
    ups, early = lax.optimization_barrier((ups, early))
    ups |= {k ^ 1: permute(v, "dp", 1) for k, v in ups.items()}
    ups |= {0: w_up[0], 1: ups_near}
    back, active, grad_pre = call(
        functools.partial(expert_kernel, cap, rows, dp_size),
        [packed] + [like((dp_size, slots, units), bf16)] * 2,
        [
            pltpu.VMEM((width, hidden_units), bf16),
            pltpu.VMEM((dp_size, slots, units), bf16),
            pltpu.VMEM((slots, P_DEV), f32),
            pltpu.VMEM((2, slots, 256 if units % 256 == 0 else 128), f32),
            pltpu.VMEM((slots, hidden_units), bf16),
            pltpu.VMEM((slots, hidden_units), bf16),
            sems((4, dp_size)),
        ],
        [got, *(ups[k] for k in range(dp_size)), early],
        4 * slots * width * hidden_units,
        raw=dp_size + 1,
        raw_outs=2,
    )
    back = swap(back)
    grads, result = call(
        functools.partial(weight_kernel, cap, rows, dp_size),
        [like((dp_size, 2, width, units), bf16), packed],
        [pltpu.VMEM((slots, hidden_units), bf16)] * 2
        + [pltpu.VMEM((width, hidden_units), bf16), sems((3, dp_size))],
        [got, tops, grad_pre, active, downs],
        6 * slots * width * hidden_units,
        raw=3,
    )
    grads, result, back = lax.optimization_barrier((grads, result, back))
    grads = lax.psum_scatter(grads, "dp", scatter_dimension=0)
    returned = swap(result)

    blocks = 1 << len(orders[0])
    parts = len(orders)
    part_width = 4 * width // parts
    rows_of = [width // blocks + 8 * (i == parts - 1) for i in range(parts)]
    half = [like((blocks // 2, rows, part_width), bf16) for rows in rows_of for _ in range(2)]
    grad_hidden, grad_rest, odd, *results = call(
        functools.partial(backward_kernel, dp_size, heads, cap),
        [like((count, width), f32), like((CLEN, width), f32)]
        + [like((dp_size // 2, P_DEV, width), bf16), like((P_DEV, width), f32)]
        + [like((P_DEV, width), bf16)] * (dp_size // 2 - 1)
        + half,
        [
            pltpu.VMEM((count, width), bf16),
            pltpu.VMEM((16, count), f32),
            pltpu.VMEM((4, P_DEV, P_DEV), f32),
            pltpu.VMEM((count, width), bf16),
            pltpu.VMEM((keys, 2 * width), bf16),
            pltpu.VMEM((width, keys), bf16),
            pltpu.VMEM((16, 3 * P_DEV), f32),
            pltpu.VMEM((parts, blocks, width // blocks + 8, part_width), bf16),
            sems((parts, 2)),
        ],
        [back, hidden, gates, pos, routes, gain_ffn, router, grad_output, kept, w_mix]
        + [query_rows, pairs, chances, normed_all, gain_attn, w_qkv],
        12 * keys * width * width + 4 * count * keys * width * 4,
        raw_outs=2 * parts,
        near=1,
    )
    even, results = results[: -2 * parts], results[-2 * parts :]
    results, returned = lax.optimization_barrier((results, returned))
    odd = permute(odd, "dp", 1)
    held = {2 * i: add(v, odd[i]) for i, v in enumerate(even)}
    for bit in bits_of(dp_size)[1:]:
        for k in [k for k in held if not k & bit]:
            held[k] = add(held[k], permute(held.pop(k | bit).astype(bf16), "dp", bit))
    grad_prompt = held[0]
    (grad_input,) = call(
        finish_kernel,
        [like((count, width), f32)],
        [],
        [block_input, gain_attn, grad_hidden, grad_prompt, grad_rest],
        10 * count * width,
    )
    (output,) = call(
        combine_kernel,
        [like((count, width), bf16)],
        [],
        [hidden, gates, pos, returned],
        4 * slots * count * width,
    )
    grad_up, grad_down = (grads[i : i + 1].astype(f32) for i in range(2))
    first = [grad_input, output, grad_up, grad_down]
    halves, first = sum_blocks([results[2 * i : 2 * i + 2] for i in range(parts)], first)
    grad_input, output, grad_up, grad_down = first
    grad_one, grad_two, grad_router, grad_table, grad_w, grad_mix = call(
        functools.partial(unpack_kernel, experts, heads),
        [like((width,), f32), like((width,), f32), like((experts, width), f32)]
        + [like((heads, 32), f32), like((width, 3 * width), f32), like((width, width), f32)],
        [
            pltpu.VMEM((parts, blocks, width // blocks + 16, part_width), bf16),
            pltpu.VMEM((width, 4 * width), f32),
            pltpu.VMEM((blocks, 8, part_width), f32),
            sems((parts, 2)),
            sems((2, blocks)),
        ],
        halves,
        0,
        raw=2 * parts,
        raw_outs=2,
    )
    return (
        output,
        grad_input,
        grad_one,
        grad_w,
        grad_mix,
        grad_table.T,
        grad_two,
        grad_router.T,
        grad_up,
        grad_down,
    )


def solution(mesh):
    in_specs = (
        P(("dp", "expert"), None),
        P(),
        P(),
        P(),
        P(),
        P(),
        P(),
        P("expert", None, "dp"),
        P("expert", None, "dp"),
        P(("dp", "expert"), None),
        P(("dp", "expert"), None),
        P(("dp", "expert"), None),
    )
    out_specs = (
        P(("dp", "expert"), None),
        P(("dp", "expert"), None),
        P(),
        P(),
        P(),
        P(),
        P(),
        P(),
        P("expert", None, "dp"),
        P("expert", None, "dp"),
    )
    return jax.shard_map(body, mesh=mesh, in_specs=in_specs, out_specs=out_specs, check_vma=False)
```

```python
import functools
import math

import jax
import jax.numpy as jnp
from jax import lax
from jax.experimental import pallas as pl
from jax.experimental.pallas import tpu as pltpu
from jax.sharding import PartitionSpec as P

CLEN = 128
P_DEV = 128

epsilon = 1e-06
masked_score = -1e30
bucket_edges = [int(math.ceil(16 * 8 ** (step / 16))) for step in range(1, 16)]
bf16 = jnp.bfloat16
f32 = jnp.float32


def contract(left, right, left_dim, right_dim):
    dims = (((left_dim,), (right_dim,)), ((), ()))
    return lax.dot_general(left, right, dims, preferred_element_type=f32)


def dot(left, right):
    return contract(left, right, 1, 0)


def dot_cols(left, right):
    return contract(left, right, 1, 1)


def dot_rows(left, right):
    return contract(left, right, 0, 0)


def iota(shape, axis):
    return lax.broadcasted_iota(jnp.int32, shape, axis)


def like(shape, dtype):
    return jax.ShapeDtypeStruct(shape, dtype)


class Load:
    def __init__(self, source, into, sem):
        self.into = into
        self.copy = pltpu.make_async_copy(source, into, sem)
        self.started = self.waited = False

    def start(self):
        if not self.started:
            self.copy.start()
            self.started = True

    def __call__(self):
        self.start()
        if not self.waited:
            self.copy.wait()
            self.waited = True
        return self.into


class Near:
    def __init__(self, ref):
        self.into = ref

    def __call__(self):
        ref = self.into
        return ref[...].reshape(1, ref.shape[0]) if len(ref.shape) == 1 else ref


def start(*loads):
    for load in loads:
        if isinstance(load, Load):
            load.start()


class Store:
    def __init__(self, ref, into, sems):
        self.ref, self.into, self.sems = ref, into, sems
        self.copies = []

    def send(self, *pieces):
        if not pieces:
            copies = [pltpu.make_async_copy(self.ref, self.into, self.sems.at[0])]
        else:
            copies = [
                pltpu.make_async_copy(self.ref.at[i], self.into.at[i], self.sems.at[at])
                for at, i in enumerate(pieces, len(self.copies))
            ]
        for copy in copies:
            copy.start()
        self.copies += copies

    def begin(self, piece):
        pltpu.make_async_copy(self.ref.at[piece], self.into.at[piece], self.sems.at[piece]).start()

    def begun(self):
        self.copies += [
            pltpu.make_async_copy(self.ref.at[i], self.into.at[i], self.sems.at[i])
            for i in range(self.ref.shape[0])
        ]

    def send_part(self, index, *part):
        source, into = self.ref.at[part], self.into.at[part]
        self.copies.append(pltpu.make_async_copy(source, into, self.sems.at[index]))
        self.copies[-1].start()


def call(body, outs, scratch, args, flops, raw=0, raw_outs=0, near=0, limit=58):
    args, outs = list(args), list(outs)
    count, results = len(args), len(outs)
    flat = [a.ndim == 1 or i < near for i, a in enumerate(args)]
    moved = [i for i in range(count - raw) if not flat[i]]
    direct = [len(o.shape) == 1 or i >= results - raw_outs for i, o in enumerate(outs)]
    pieces = 32

    def kernel(*refs):
        given, refs = refs[:count], refs[count:]
        made, refs = refs[:results], refs[results:]
        held, refs = refs[: len(moved)], refs[len(moved) :]
        ready, refs = refs[: results - sum(direct)], refs[results - sum(direct) :]
        in_sems, out_sems, *rest = refs
        loads = []
        for i in range(count):
            if i in moved:
                at = moved.index(i)
                loads.append(Load(given[i], held[at], in_sems.at[at]))
            elif flat[i]:
                loads.append(Near(given[i]))
            else:
                loads.append(given[i])
        ready = iter(ready)
        stores = [
            made[i] if direct[i] else Store(next(ready), made[i], out_sems.at[i])
            for i in range(results)
        ]
        body(loads, stores, *rest)
        for load in loads:
            if isinstance(load, Load):
                load()
        stores = [store for store in stores if isinstance(store, Store)]
        for store in stores:
            if not store.copies:
                store.send()
        for store in stores:
            for copy in store.copies:
                copy.wait()

    held = [args[i] for i in moved] + [o for o, is_direct in zip(outs, direct) if not is_direct]
    sems = pltpu.SemaphoreType.DMA
    size = sum(math.prod(a.shape) * a.dtype.itemsize for a in args + outs)
    room = [pltpu.VMEM(a.shape, a.dtype) for a in held]
    made = pl.pallas_call(
        kernel,
        out_shape=outs,
        in_specs=[pl.BlockSpec(memory_space=pltpu.VMEM if f else pl.ANY) for f in flat],
        out_specs=[
            pl.BlockSpec(memory_space=pltpu.VMEM if len(o.shape) == 1 else pl.ANY) for o in outs
        ],
        scratch_shapes=room + [sems((max(len(moved), 1),)), sems((results, pieces))] + scratch,
        compiler_params=pltpu.CompilerParams(vmem_limit_bytes=limit << 20),
        cost_estimate=pl.CostEstimate(flops=flops, bytes_accessed=size, transcendentals=0),
    )(*args)
    return list(made)


def bucket_of(distance):
    beyond = sum(((distance >= edge).astype(jnp.int32) for edge in bucket_edges))
    return jnp.clip(jnp.where(distance < 16, distance, 16 + beyond), 0, 31)


def thirds(value):
    high = value.astype(bf16).astype(f32)
    mid = (value - high).astype(bf16).astype(f32)
    return high, mid, value - high - mid


def pieces_of(value, count=3):
    return [v.astype(bf16) for v in thirds(value)[:count]]


def norm_rows(values):
    return lax.rsqrt(jnp.mean(values * values, axis=-1, keepdims=True) + epsilon)


def columns_of(lines):
    count = lines[0].shape[1]
    lines = [line.astype(f32) for line in lines]
    lines += [jnp.zeros((8 - len(lines), count), f32)]
    columns = jnp.transpose(jnp.concatenate(lines, axis=0))
    return [columns[:, c : c + 1] for c in range(len(lines) - 1)]


def route_kernel(experts, cap, rows, loads, stores):
    routes, fill_order, grad_out = loads
    pos, sent = stores
    start(*loads)
    routes = routes()[...]
    count = routes.shape[1]
    order = jnp.broadcast_to(fill_order()[...], (16, 2 * count))
    coarse = order & ~31
    order = jnp.where(iota(order.shape, 0) < 8, coarse, order - coarse).astype(f32).astype(bf16)
    at, to = iota((2 * count, 2 * count), 0), iota((2 * count, 2 * count), 1)
    pick = (at == jnp.where(to < count, 2 * to, 2 * (to - count) + 1)).astype(f32).astype(bf16)
    order = dot(order, pick)
    order = order[:8] + order[8:]
    orow = [order[:1, :count], order[:1, count:]]
    row = [routes[c : c + 1, :].astype(f32) for c in range(2)]
    col = columns_of([*row, *orow])
    col, ocol = col[:2], col[2:]
    slots = []
    for c in range(2):
        rank = jnp.zeros((1, count), f32)
        for other in range(2):
            hit = (col[other] == row[c]) & (ocol[other] < orow[c])
            rank += jnp.sum(hit.astype(f32), axis=0, keepdims=True)
        rank = rank.astype(jnp.int32)
        slot = routes[c : c + 1, :] * rows + rank
        slots.append(jnp.where(rank < cap, slot, -1))
    pos.ref[...] = jnp.concatenate([*slots, jnp.zeros((6, count), jnp.int32)], axis=0)
    pos.send()
    grad_top = grad_out()[...]
    for k in range(experts):
        index = iota((rows, count), 0) + k * rows
        onehot = ((index == slots[0]) | (index == slots[1])).astype(f32).astype(bf16)
        at = slice(k * rows, (k + 1) * rows)
        sent.ref[at, :] = dot(onehot, grad_top).astype(bf16)
        sent.send_part(k, at)


def bias_tiles(table, tiles):
    heads, buckets = table.shape
    width = 2 * P_DEV
    onehot = (bucket_of(iota((buckets, width), 1)) == iota((buckets, width), 0)).astype(f32)
    line = sum(dot(part, onehot.astype(bf16)) for part in pieces_of(table))
    causal = iota((P_DEV, P_DEV), 1) >= iota((P_DEV, P_DEV), 0)
    for h in range(heads):
        spread = jnp.broadcast_to(line[h : h + 1, :], (P_DEV, width))
        rolled = pltpu.roll(spread, 0, 1, stride=1, stride_axis=0)
        tiles[h, 0] = jnp.full((P_DEV, P_DEV), masked_score, f32)
        tiles[h, 1] = jnp.where(causal, rolled[:, :P_DEV], masked_score)
        tiles[h, 2] = rolled[:, P_DEV:]
        tiles[h, 3] = jnp.broadcast_to(line[h : h + 1, width - 1 : width], (P_DEV, P_DEV))


def tile_index(block, dp_size, dp_index, continuation):
    if block == 0:
        return 1 if continuation else 0
    key = dp_index ^ (block - 1)
    if continuation:
        return jnp.minimum(dp_size - key, 2) + 1
    if block == 1:
        return 1
    return jnp.clip(dp_index - key, -1, 2) + 1


def attend_kernel(dp_size, heads, cap, rows, experts, loads, stores, tiles, scores):
    x, *others, w_qkv, gain, table, w_mix, gain_ffn, router, routes, pos = loads
    hidden, kept, gates, chances, pairs, query_rows, normed_all, sent = stores
    start(x, table, *others, w_qkv)
    count, width = x.into.shape
    head_size = width // heads
    dp_index = lax.axis_index("dp")
    values = x()[...].astype(f32)
    low = values * norm_rows(values) * gain()
    normed_all.ref[0:CLEN, :] = low[P_DEV:].astype(bf16)
    normed_all.ref[CLEN:count, :] = low[:P_DEV].astype(bf16)
    for k, other in enumerate(others):
        values = other()[...].astype(f32)
        at = slice((k + 2) * P_DEV, (k + 3) * P_DEV)
        normed_all.ref[at, :] = (values * norm_rows(values) * gain()).astype(bf16)
    normed_all.send()
    bias_tiles(table()[...], tiles)
    pairs, queries, chance = pairs, query_rows.ref, chances.ref
    weights = w_qkv()
    start(w_mix, router, routes, pos)
    queries[...] = dot(normed_all.ref[:count, :], weights[:, :width]).astype(bf16)
    query_rows.send()
    pairs.ref[...] = dot(normed_all.ref[...], weights[:, width:]).astype(bf16)
    pairs.send()
    left = iota((count, P_DEV), 1) < head_size
    for p in range(heads // 2):
        cut = slice(p * P_DEV, (p + 1) * P_DEV)
        key = pairs.ref[:, cut]
        value_t = jnp.transpose(pairs.ref[:, width + p * P_DEV : width + (p + 1) * P_DEV])
        query = queries[:, cut] * bf16(head_size**-0.5)
        zero = jnp.zeros_like(query)
        parts = []
        for s in range(2):
            h = 2 * p + s
            part = jnp.where(left, query, zero) if s == 0 else jnp.where(left, zero, query)
            raw = dot_cols(key, part)
            top = None
            for b in range(dp_size + 1):
                bias = jnp.concatenate(
                    [
                        tiles[h, tile_index(b, dp_size, dp_index, True)],
                        tiles[h, tile_index(b, dp_size, dp_index, False)],
                    ],
                    axis=1,
                )
                block = raw[b * P_DEV : (b + 1) * P_DEV, :] + bias
                scores[s, b * P_DEV : (b + 1) * P_DEV, :] = block
                most = jnp.max(block, axis=0, keepdims=True)
                top = most if top is None else jnp.maximum(top, most)
            total = jnp.zeros((1, count), f32)
            for b in range(dp_size + 1):
                weight = jnp.exp(scores[s, b * P_DEV : (b + 1) * P_DEV, :] - top)
                scores[s, b * P_DEV : (b + 1) * P_DEV, :] = weight
                total += jnp.sum(weight, axis=0, keepdims=True)
            inverse = 1.0 / total
            chance[h, :, :] = (scores[s] * inverse).astype(bf16)
            parts.append(dot(value_t[s * head_size : (s + 1) * head_size, :], chance[h]))
        part = jnp.transpose(jnp.concatenate(parts, axis=0))
        kept.ref[P_DEV:, cut] = part[:CLEN]
        kept.ref[:P_DEV, cut] = part[CLEN:]
        chances.send(2 * p, 2 * p + 1)
    kept.send()
    hid = x()[...].astype(f32) + dot(kept.ref[...].astype(bf16), w_mix()[...])
    hidden.ref[...] = hid
    hidden.send()
    normed_two = hid * norm_rows(hid) * gain_ffn()
    weights = jnp.concatenate([v.astype(f32) for v in pieces_of(router()[...])], axis=0).astype(bf16)
    logits = sum(dot_cols(weights, part) for part in pieces_of(normed_two, 2))
    logits = logits[:experts] + logits[experts : 2 * experts] + logits[2 * experts :]
    row = iota(logits.shape, 0)
    routes = routes()[...]
    pick = [
        jnp.sum(jnp.where(row == routes[c : c + 1, :], logits, 0.0), axis=0, keepdims=True)
        for c in range(2)
    ]
    most = jnp.maximum(pick[0], pick[1])
    raised = [jnp.exp(v - most) for v in pick]
    gate = [v / (raised[0] + raised[1]) for v in raised]
    gates.ref[...] = jnp.concatenate([*gate, jnp.zeros((6, count), f32)], axis=0)
    gates.send()
    pos = pos()[...]
    pos_col = columns_of([pos[c : c + 1, :] for c in range(2)])
    pos_col = [v.astype(jnp.int32) for v in pos_col]
    gate = columns_of(gate)
    lane = iota((count, P_DEV), 1)
    low = normed_two.astype(bf16)
    for k in range(experts):
        index = iota((rows, count), 0) + k * rows
        onehot = (index == pos[0:1, :]) | (index == pos[1:2, :])
        block = dot(onehot.astype(f32).astype(bf16), low)
        line = jnp.zeros((1, P_DEV), f32)
        for c in range(2):
            mine = pos_col[c] == lane + k * rows
            line += jnp.sum(jnp.where(mine, gate[c], 0.0), axis=0, keepdims=True)
        line = jnp.concatenate([*thirds(line), jnp.zeros((1, width - 3 * P_DEV), f32)], axis=1)
        at = slice(k * rows, (k + 1) * rows)
        sent.ref[at, :] = jnp.where(iota((rows, width), 0) == cap, line, block).astype(bf16)
        sent.send_part(k, at)


def gelu_parts(value):
    factor = math.sqrt(2 / math.pi)
    square = value * value
    bend = jnp.tanh(factor * value * (1.0 + 0.044715 * square))
    half = 0.5 * (1.0 + bend)
    slope = half + (0.5 * factor) * value * (1.0 - bend * bend) * (1.0 + 0.134145 * square)
    return value * half, slope


def gather_columns(blocks, into, sems):
    width = into.shape[1] // len(blocks)
    return [
        Load(block, into.at[:, i * width : (i + 1) * width], sems.at[i])
        for i, block in enumerate(blocks)
    ]


def early_kernel(loads, stores, down, early, sems):
    tops, downs = loads
    dp_index = lax.axis_index("dp")
    blocks, width, units = downs.shape
    copies = gather_columns([downs.at[q ^ dp_index] for q in range(blocks)], down, sems.at[0])
    sent = []
    start(tops, *copies[:2])
    for q in range(blocks):
        at = slice(q * units, (q + 1) * units)
        copies[q]()
        start(*copies[q + 1 : q + 3])
        early[q] = dot(tops()[...], down[:, at]).astype(bf16)
        sent.append(pltpu.make_async_copy(early.at[q], stores[0].at[q], sems.at[1, q]))
        sent[-1].start()
    for copy in sent:
        copy.wait()


def payload_line(block, cap, index):
    rows = block.shape[0]
    line = block[rows - 16 :, index * P_DEV : (index + 1) * P_DEV].astype(f32)
    return line[cap - rows + 16 : cap - rows + 17, :]


def gate_column(block, cap):
    line = sum(payload_line(block, cap, i) for i in range(3))
    same = iota((block.shape[0], P_DEV), 0) == iota((block.shape[0], P_DEV), 1)
    return jnp.sum(jnp.where(same, line, 0.0), axis=1, keepdims=True)


def expert_kernel(cap, rows, blocks, loads, stores, up, early, total, product, active, grad_pre, sems):
    got = loads[0]
    back, *kept = stores
    slots, width = got.into.shape
    units = up.shape[1] // blocks
    start(got)

    def fetch(q):
        cut = slice(q * units, (q + 1) * units)
        pltpu.make_async_copy(loads[1 + q], up.at[:, cut], sems.at[0, q]).start()
        pltpu.make_async_copy(loads[-1].at[q], early.at[q], sems.at[1, q]).start()

    fetch(0)
    pieces = [slice(at, at + rows) for at in range(0, slots, rows)]
    same = iota((rows, P_DEV), 0) == iota((rows, P_DEV), 1)
    gates = [gate_column(got()[at, :], cap) for at in pieces]
    chunk = product.shape[2]
    total[...] = jnp.zeros_like(total)
    def step(q, carry):
        base = pl.multiple_of(q*units, units)
        pltpu.make_async_copy(loads[1], up.at[:, pl.ds(base, units)], sems.at[0,q]).wait()
        pltpu.make_async_copy(loads[-1].at[q], early.at[q], sems.at[1,q]).wait()
        for after_q in range(1, blocks):
            pl.when(q + 1 == after_q)(functools.partial(fetch, after_q))
        for i in range(units//chunk):
            to = pl.ds(pl.multiple_of(base + i*chunk, chunk), chunk)
            product[i % 2] = dot(got()[...], up[:, to])
            for at, gate in zip(pieces, gates):
                low, slope = gelu_parts(product[i % 2, at, :])
                active[at, to] = low.astype(bf16)
                grad = early[q, at, i * chunk : (i + 1) * chunk].astype(f32)
                both = grad * low
                total[at, :] += sum(both[:, j : j + P_DEV] for j in range(0, chunk, P_DEV))
                grad_pre[at, to] = (grad * slope * gate).astype(bf16)
        for i, part in enumerate((active, grad_pre)):
            pltpu.make_async_copy(part.at[:, pl.ds(base, units)], kept[i].at[q], sems.at[2 + i, q]).start()
        return carry
    lax.fori_loop(0, blocks, step, 0)
    half = len(pieces) // 2 * rows
    value = [dot_cols(grad_pre[i : i + half, :], up[...]) for i in (0, half)]
    for k, at in enumerate(pieces):
        line = jnp.sum(total[at, :], axis=1, keepdims=True)
        line = jnp.sum(jnp.where(same, line, 0.0), axis=0, keepdims=True)
        line = [*thirds(line), jnp.zeros((1, width - 3 * P_DEV), f32)]
        line = jnp.concatenate(line, axis=1)
        part = value[at.start // half][at.start % half :][:rows]
        back.ref[at, :] = jnp.where(iota((rows, width), 0) == cap, line, part).astype(bf16)
        back.send_part(k, at)
    for q in range(blocks):
        for i, part in enumerate((active, grad_pre)):
            pltpu.make_async_copy(part.at[:, q*units:(q+1)*units], kept[i].at[q], sems.at[2 + i, q]).wait()

def weight_kernel(cap, rows, blocks, loads, stores, grad_pre, active, down, sems):
    got, tops, *whole, downs = loads
    dp_index = lax.axis_index("dp")
    start(got, tops)
    units = active.shape[1] // blocks

    def copies_of(q):
        cut = pl.ds(pl.multiple_of(q * units, units), units)
        sources = (whole[0].at[q], whole[1].at[q], downs.at[q ^ dp_index])
        return [
            pltpu.make_async_copy(source, into.at[:, cut], sems.at[i, q])
            for i, (source, into) in enumerate(zip(sources, (grad_pre, active, down)))
        ]

    for q in range(blocks):
        for copy in copies_of(q):
            copy.start()
    grads, result = stores
    grad_out = []
    for at in range(0, got.into.shape[0], rows):
        gate = gate_column(got()[at : at + rows, :], cap)
        grad_out.append((gate * tops()[at : at + rows, :].astype(f32)).astype(bf16))
    rows_t = jnp.transpose(got()[...])
    grad_t = jnp.transpose(jnp.concatenate(grad_out, axis=0))

    def step(q, carry):
        for copy in copies_of(q):
            copy.wait()
        cut = pl.ds(pl.multiple_of(q * units, units), units)
        grads.ref[q ^ dp_index, 0] = dot(rows_t, grad_pre[:, cut]).astype(bf16)
        grads.ref[q ^ dp_index, 1] = dot(grad_t, active[:, cut]).astype(bf16)
        grads.begin(q ^ dp_index)
        return carry

    lax.fori_loop(0, blocks, step, 0)
    grads.begun()
    result.ref[...] = dot_cols(active[...], down[...]).astype(bf16)


def combine_kernel(loads, stores):
    hidden, gates, pos, back = loads
    (output,) = stores
    start(*loads)
    columns = columns_of([gates()[0:1, :], gates()[1:2, :], pos()[0:1, :], pos()[1:2, :]])
    held = back()[...]
    index = iota((hidden.into.shape[0], held.shape[0]), 1)
    total = hidden()[...]
    for c in range(2):
        onehot = (index == columns[2 + c].astype(jnp.int32)).astype(f32).astype(bf16)
        total += columns[c] * dot(onehot, held)
    output.ref[...] = total.astype(bf16)


def diagonal_sums(values):
    size, width = values.shape
    while size > 8:
        size //= 2
        values = values[:size] + pltpu.roll(values[size:], width - size, 1)
    row = iota(values.shape, 0)
    for bit in (4, 2, 1):
        values = jnp.where((row & bit) != 0, pltpu.roll(values, width - bit, 1), values)
    return jnp.sum(values, axis=0, keepdims=True)


def backward_kernel(dp_size, heads, cap, loads, stores, grad_att, delta, sums, grad_query,
                    grad_pairs, normed_t, lines, staged, sems):
    back, hidden, gates, pos, routes, gain_ffn, router, grad_output, kept, w_mix = loads[:10]
    query_rows, pairs, chances, normed_all, gain, w_qkv = loads[10:]
    start(back, gates, pos, routes, hidden, router, grad_output, kept, w_mix)
    experts = router.into.shape[0]
    rows = back.into.shape[0] // experts
    (grad_hidden, grad_rest, grad_odd), stores = stores[:3], stores[3:]
    parts = staged.shape[0]
    grad_even, halves = stores[: -2 * parts], stores[-2 * parts :]
    mine = [block_index(order) for order in orders]
    width = hidden.into.shape[1]
    blocks, step_rows, part_width = staged.shape[1], width // staged.shape[1], staged.shape[3]
    copies = []

    def put(first, value):
        for at in range(0, value.shape[1], 256):
            index, into = divmod(first + at, part_width)
            for p in range(blocks):
                part = value[p * step_rows : (p + 1) * step_rows, at : at + 256]
                to = slice(into, into + 256)
                staged[index, p ^ mine[index], 0:step_rows, to] = part.astype(bf16)

    def send(index, small=()):
        half = blocks // 2
        count = step_rows + (8 if small else 0)
        for p in range(blocks if small else 0):
            more = small[p] if p < len(small) else jnp.zeros((8, width), f32)
            staged[index, p ^ mine[index], step_rows:, 0:width] = more.astype(bf16)
        for i in range(2):
            source = staged.at[index, i * half : (i + 1) * half, 0:count]
            into = halves[2 * index + i]
            copies.append(pltpu.make_async_copy(source, into, sems.at[index, i]))
            copies[-1].start()

    count, width = hidden.into.shape
    head_size = width // heads
    given = [gates()[0:1, :], gates()[1:2, :]]
    given += [ref[c : c + 1, :] for ref in (pos(), routes()) for c in range(2)]
    columns = columns_of(given)
    gate = columns[:2]
    pos, routes = ([v.astype(jnp.int32) for v in columns[i : i + 2]] for i in (2, 4))
    index = iota((count, experts * rows), 1)
    onehot = (index == pos[0]) | (index == pos[1])
    grad_two = dot(onehot.astype(f32).astype(bf16), back()[...])
    lane = iota((count, P_DEV), 1)
    found = [jnp.zeros((count, P_DEV), f32) for c in range(2)]
    for k in range(experts):
        line = sum(payload_line(back()[k * rows : (k + 1) * rows, :], cap, i) for i in range(3))
        for c in range(2):
            found[c] += jnp.where(pos[c] == lane + k * rows, line, 0.0)
    grad_gate = [jnp.sum(v, axis=1, keepdims=True) for v in found]
    hid = hidden()[...]
    start(query_rows, pairs, chances)
    scale = norm_rows(hid)
    normed_two = hid * scale * gain_ffn()
    slope = gate[0] * gate[1] * (grad_gate[0] - grad_gate[1])
    lane = iota((count, experts), 1)
    grad_logits = jnp.where(lane == routes[0], slope, 0.0) - jnp.where(lane == routes[1], slope, 0.0)
    left = thirds(grad_logits)
    right = thirds(router()[...])
    pairs_of = [(0, 0), (0, 1), (1, 0), (0, 2), (1, 1), (2, 0)]
    left_all = jnp.concatenate([left[i] for i, _ in pairs_of], axis=1).astype(bf16)
    right_all = jnp.concatenate([right[i] for _, i in pairs_of], axis=0).astype(bf16)
    grad_two += dot(left_all, right_all)
    left = jnp.transpose(jnp.concatenate(left, axis=1)).astype(bf16)
    grad_router = sum(dot(left, part) for part in pieces_of(normed_two, 2))
    grad_router = grad_router[:experts] + grad_router[experts : 2 * experts] + grad_router[2 * experts :]
    grad_gain_ffn = jnp.sum(grad_two * hid * scale, axis=0, keepdims=True)
    weighted = grad_two * gain_ffn()
    inner = jnp.mean(weighted * hid, axis=-1, keepdims=True)
    grad_hid = grad_output()[...].astype(f32) + scale * weighted - hid * (scale**3 * inner)
    grad_hidden.ref[...] = grad_hid
    grad_hidden.send()
    mixed = grad_hid.astype(bf16)
    att = kept()[...]
    weights = w_mix()[...]
    start(normed_all, w_qkv)
    top = dot_cols(mixed, weights).astype(bf16)
    grad_att[0:CLEN, :] = top[P_DEV:]
    grad_att[CLEN:, :] = top[:P_DEV]
    put(3 * width, dot_rows(att.astype(bf16), mixed))
    prod_t = jnp.transpose(top.astype(f32) * att)
    for h in range(heads):
        line = prod_t[h * head_size : (h + 1) * head_size, :]
        line = jnp.sum(line, axis=0, keepdims=True)
        delta[h : h + 1, :] = jnp.concatenate([line[:, P_DEV:], line[:, :P_DEV]], axis=1)
    dp_index = lax.axis_index("dp")
    left = iota((count, P_DEV), 1) < head_size
    left_keys = iota((pairs.into.shape[0], P_DEV), 1) < head_size
    lines[...] = jnp.zeros_like(lines)
    queries, pairs_ref, chances = query_rows(), pairs(), chances()
    for p in range(heads // 2):
        cut = slice(p * P_DEV, (p + 1) * P_DEV)
        cut_value = slice(width + p * P_DEV, width + (p + 1) * P_DEV)
        key_t = jnp.transpose(pairs_ref[:, cut])
        value = pairs_ref[:, cut_value]
        query = queries[:, cut] * bf16(head_size**-0.5)
        top = grad_att[:, cut]
        zero = jnp.zeros_like(top)
        grad_q, grad_k, grad_v = [], [], []
        for s in range(2):
            h = 2 * p + s
            part = jnp.where(left, top, zero) if s == 0 else jnp.where(left, zero, top)
            grad_chance = dot_cols(value, part)
            chance = chances[h]
            grad_score = (chance.astype(f32) * (grad_chance - delta[h : h + 1, :])).astype(bf16)
            grad_v.append(dot(chance, top))
            grad_k.append(dot(grad_score, query))
            grad_q.append(dot(key_t[s * head_size : (s + 1) * head_size, :], grad_score))
            sums[...] = jnp.zeros_like(sums)
            for b in range(dp_size + 1):
                tile = grad_score[b * P_DEV : (b + 1) * P_DEV, :].astype(f32)
                sums[tile_index(b, dp_size, dp_index, True)] += tile[:, :P_DEV]
                if b > 0:
                    sums[tile_index(b, dp_size, dp_index, False)] += tile[:, P_DEV:]
            both = jnp.concatenate([sums[1], sums[2]], axis=1)
            lines[h : h + 1, : 2 * P_DEV] = diagonal_sums(both)
            lines[h : h + 1, 2 * P_DEV :] = jnp.sum(sums[3], axis=0, keepdims=True)
        grad_pairs[:, cut] = jnp.where(left_keys, grad_k[0], grad_k[1]).astype(bf16)
        grad_pairs[:, cut_value] = jnp.where(left_keys, grad_v[0], grad_v[1]).astype(bf16)
        grad_q = jnp.transpose(jnp.concatenate(grad_q, axis=0) * head_size**-0.5)
        grad_query[:, cut] = grad_q.astype(bf16)
    normed_all = normed_all()
    normed_t[...] = jnp.transpose(normed_all[...])
    w_qkv = w_qkv()
    grad_low = dot_cols(grad_pairs[...], w_qkv[:, width:])
    for k in range(1, dp_size):
        part = grad_low[(k + 1) * P_DEV : (k + 2) * P_DEV].astype(bf16)
        if k % 2:
            grad_odd.ref[k // 2] = part
        else:
            grad_even[k // 2].ref[...] = part
            grad_even[k // 2].send()
    grad_odd.send()
    own = grad_low[:count] + dot_cols(grad_query[...], w_qkv[:, :width])
    grad_rest.ref[...] = own[:CLEN]
    grad_rest.send()
    grad_even[0].ref[...] = own[CLEN:]
    grad_even[0].send()
    grad_gain = jnp.sum(own * normed_all[:count, :].astype(f32), axis=0, keepdims=True)
    grad_gain += jnp.sum(
        grad_low[count:] * normed_all[count:, :].astype(f32), axis=0, keepdims=True
    )
    grad_gain = grad_gain / gain()
    distance = iota((lines.shape[1], P_DEV), 0)
    bucket = jnp.where(distance < 2 * P_DEV, bucket_of(distance), 31)
    onehot = (bucket == iota((lines.shape[1], P_DEV), 1)).astype(f32).astype(bf16)
    table = sum(dot(part, onehot) for part in pieces_of(lines[...]))
    table = jnp.concatenate([table, jnp.zeros((16, width - P_DEV), f32)], axis=1)
    row = iota((8, width), 0)
    small = [jnp.where(row == 0, grad_gain, jnp.where(row == 1, grad_gain_ffn, 0.0))]
    small += [table[:8], table[8:]]
    small += [grad_router[i : i + 8] for i in range(0, experts, 8)]
    put(0, dot(normed_t[:, :count], grad_query[...]))
    put(width, dot(normed_t[...], grad_pairs[:, :width]))
    send(0)
    put(2 * width, dot(normed_t[...], grad_pairs[:, width:]))
    send(1)
    send(2, small)
    for copy in copies:
        copy.wait()


def unpack_kernel(experts, heads, loads, stores, held, staged, small, sems_in, sems):
    gain_one, gain_two, router, table, grad_w, grad_mix = stores
    half, _, part_width = loads[0].shape
    parts = len(loads) // 2
    width, rows = grad_mix.shape[1], staged.shape[0] // (2 * half)
    halves = []
    for index in range(parts):
        count = loads[2 * index].shape[1]
        for j in range(2):
            into = held.at[index, j * half : (j + 1) * half, 0:count]
            halves.append(Load(loads[2 * index + j], into, sems_in.at[index, j]))
    start(*halves[0::2], *halves[1::2])
    mine = [block_index(order) for order in orders]
    copies = []
    for j in range(2 * half):
        if j % half == 0:
            for load in halves[j // half :: 2]:
                load()
        p = j ^ (mine[0] // half * half)
        at = pl.ds(pl.multiple_of(p * rows, rows), rows)
        to = slice(j * rows, (j + 1) * rows)
        for index in range(parts):
            place = j // half * half + ((j ^ mine[index]) % half)
            block = held[index, place].astype(f32)
            staged[to, index * part_width : (index + 1) * part_width] = block[:rows]
        small[p] = block[rows : rows + 8]
        for i, into in enumerate((grad_w, grad_mix)):
            cut = slice(0, 3 * width) if i == 0 else slice(3 * width, 4 * width)
            copies.append(pltpu.make_async_copy(staged.at[to, cut], into.at[at], sems.at[i, j]))
            copies[-1].start()
    gain_one[...] = small[0, 0, :width]
    gain_two[...] = small[0, 1, :width]
    lines = jnp.concatenate([small[1], small[2]], axis=0)
    table.ref[...] = lines[:heads, :32]
    for i in range(experts // 8):
        router.ref[i * 8 : (i + 1) * 8, :] = small[3 + i][:, :width]
    for copy in copies:
        copy.wait()


def finish_kernel(loads, stores):
    x, gain, grad_hidden, grad_prompt, grad_rest = loads
    start(*loads)
    values = x()[...].astype(f32)
    scale = norm_rows(values)
    grad = jnp.concatenate([grad_prompt()[...], grad_rest()[...]], axis=0)
    weighted = grad * gain()
    inner = jnp.mean(weighted * values, axis=-1, keepdims=True)
    stores[0].ref[...] = grad_hidden()[...] + scale * weighted - values * (scale**3 * inner)


def permute(value, axis, offset):
    size = lax.axis_size(axis)
    return lax.ppermute(value, axis, [(i, i ^ offset) for i in range(size)])


def bits_of(size):
    return [1 << b for b in range(size.bit_length() - 1)]


def spread_far(block):
    held = {0: block}
    for bit in bits_of(lax.axis_size("dp"))[:0:-1]:
        held.update({k ^ bit: permute(v, "dp", bit) for k, v in list(held.items())})
    return held


def spread_near(held):
    held = held | {k ^ 1: permute(v, "dp", 1) for k, v in held.items()}
    return [held[k] for k in sorted(held)]


def swap(blocks):
    return lax.all_to_all(blocks, "expert", split_axis=0, concat_axis=0, tiled=True)


def add(left, right):
    return left.astype(f32) + right.astype(f32)


def after(value, *first):
    return lax.optimization_barrier((value, *first))[0]


halving = {"c": ("dp", 1), "x": ("dp", 2), "y": ("expert", 1), "z": ("expert", 2)}
orders = ["cyzx", "czyx", "cyzx"]
widening = ["zxy", "xyz", "yzx"]


def block_index(order):
    index = jnp.int32(0)
    for name in order:
        axis, bit = halving[name]
        index = index * 2 + (lax.axis_index(axis) & bit) // bit
    return index


def halve(keep, send, order):
    for name in order[:-1]:
        blocks = add(keep, permute(send, *halving[name])).astype(bf16)
        half = blocks.shape[0] // 2
        keep, send = blocks[:half], blocks[half:]
    return add(keep, permute(send, *halving[order[-1]])).astype(bf16)


def widen(blocks, order, back):
    for name in back:
        more = permute(blocks, *halving[name])
        blocks = jnp.concatenate([blocks, more], axis=order.index(name))
    return blocks


def other_steps():
    return [(axis, bit) for axis in ("dp", "expert") for bit in bits_of(lax.axis_size(axis))
            if (axis, bit) not in halving.values()]


def sum_blocks(parts, first):
    parts = [halve(*part, order) for part, order in zip(parts, orders)]
    whole = jnp.concatenate(parts, axis=1)
    for step in other_steps():
        whole = add(whole, permute(whole, *step)).astype(bf16)
    wide = []
    at = 0
    for part, order, back in zip(parts, orders, widening):
        block = whole[:, at : at + part.shape[1]]
        block = block.reshape((1,) * len(order) + block.shape[1:])
        wide.append(widen(block, order, back[:-1]))
        at += part.shape[1]
    wide[-1], first = lax.optimization_barrier((wide[-1], first))
    halves = []
    for block, order, back in zip(wide, orders, widening):
        block = widen(block, order, back[-1:])
        block = block.reshape(-1, *block.shape[-2:])
        halves += [block, permute(block, *halving[order[0]])]
    return halves, first


def body(
    block_input,
    gain_attn,
    w_qkv,
    w_mix,
    rel_bias,
    gain_ffn,
    w_router,
    w_up,
    w_down,
    routes,
    fill_order,
    grad_output,
):
    count, width = block_input.shape
    heads = rel_bias.shape[1]
    dp_size = lax.axis_size("dp")
    experts = w_router.shape[1]
    cap = 9 * 2 * count // (8 * experts)
    rows = (cap + 16) // 16 * 16
    slots = experts * rows
    keys = (dp_size + 1) * P_DEV
    units = w_up.shape[2]
    hidden_units = units * dp_size
    routes, router = routes.T, w_router.T
    packed = like((slots, width), bf16)

    others = spread_far(block_input[:P_DEV])
    downs = lax.all_gather(w_down[0], "dp", axis=0)
    pos, tops = call(
        functools.partial(route_kernel, experts, cap, rows),
        [like((8, count), jnp.int32), packed],
        [],
        [routes, fill_order, grad_output],
        2 * slots * count * width,
    )
    tops, others = lax.optimization_barrier((tops, others))
    tops = swap(tops)
    others = spread_near(others)[1:]
    hidden, kept, gates, chances, pairs, query_rows, normed_all, sent = call(
        functools.partial(attend_kernel, dp_size, heads, cap, rows, experts),
        [
            like((count, width), f32),
            like((count, width), f32),
            like((8, count), f32),
            like((heads, keys, count), bf16),
            like((keys, 2 * width), bf16),
            like((count, width), bf16),
            like((keys, width), bf16),
            packed,
        ],
        [
            pltpu.VMEM((heads, 4, P_DEV, P_DEV), f32),
            pltpu.VMEM((2, keys, count), f32),
        ],
        [block_input, *others, w_qkv, gain_attn, rel_bias.T, w_mix, gain_ffn, router]
        + [routes, pos],
        4 * keys * width * width + 4 * count * keys * width * 2,
    )
    sems = pltpu.SemaphoreType.DMA
    (early,) = call(
        early_kernel,
        [like((dp_size, slots, units), bf16)],
        [
            pltpu.VMEM((width, hidden_units), bf16),
            pltpu.VMEM((dp_size, slots, units), bf16),
            sems((2, dp_size)),
        ],
        [tops, downs],
        2 * slots * width * hidden_units,
        raw=1,
        raw_outs=1,
    )
    w_near, w_far, sent = lax.optimization_barrier((w_up, w_up, sent))
    got = swap(sent)
    ups = spread_far(w_far[0])
    del ups[0]
    ups, early = lax.optimization_barrier((ups, early))
    ups |= {k ^ 1: permute(v, "dp", 1) for k, v in ups.items()}
    ups |= {0: w_up[0], 1: permute(w_near[0], "dp", 1)}
    back, active, grad_pre = call(
        functools.partial(expert_kernel, cap, rows, dp_size),
        [packed] + [like((dp_size, slots, units), bf16)] * 2,
        [
            pltpu.VMEM((width, hidden_units), bf16),
            pltpu.VMEM((dp_size, slots, units), bf16),
            pltpu.VMEM((slots, P_DEV), f32),
            pltpu.VMEM((2, slots, 256 if units % 256 == 0 else 128), f32),
            pltpu.VMEM((slots, hidden_units), bf16),
            pltpu.VMEM((slots, hidden_units), bf16),
            sems((4, dp_size)),
        ],
        [got, *(ups[k] for k in range(dp_size)), early],
        4 * slots * width * hidden_units,
        raw=dp_size + 1,
        raw_outs=2,
    )
    back = swap(back)
    grads, result = call(
        functools.partial(weight_kernel, cap, rows, dp_size),
        [like((dp_size, 2, width, units), bf16), packed],
        [pltpu.VMEM((slots, hidden_units), bf16)] * 2
        + [pltpu.VMEM((width, hidden_units), bf16), sems((3, dp_size))],
        [got, tops, grad_pre, active, downs],
        6 * slots * width * hidden_units,
        raw=3,
    )
    grads, result, back = lax.optimization_barrier((grads, result, back))
    grads = lax.psum_scatter(grads, "dp", scatter_dimension=0)
    returned = swap(result)

    blocks = 1 << len(orders[0])
    parts = len(orders)
    part_width = 4 * width // parts
    rows_of = [width // blocks + 8 * (i == parts - 1) for i in range(parts)]
    half = [like((blocks // 2, rows, part_width), bf16) for rows in rows_of for _ in range(2)]
    grad_hidden, grad_rest, odd, *results = call(
        functools.partial(backward_kernel, dp_size, heads, cap),
        [like((count, width), f32), like((CLEN, width), f32)]
        + [like((dp_size // 2, P_DEV, width), bf16), like((P_DEV, width), f32)]
        + [like((P_DEV, width), bf16)] * (dp_size // 2 - 1)
        + half,
        [
            pltpu.VMEM((count, width), bf16),
            pltpu.VMEM((16, count), f32),
            pltpu.VMEM((4, P_DEV, P_DEV), f32),
            pltpu.VMEM((count, width), bf16),
            pltpu.VMEM((keys, 2 * width), bf16),
            pltpu.VMEM((width, keys), bf16),
            pltpu.VMEM((16, 3 * P_DEV), f32),
            pltpu.VMEM((parts, blocks, width // blocks + 8, part_width), bf16),
            sems((parts, 2)),
        ],
        [back, hidden, gates, pos, routes, gain_ffn, router, grad_output, kept, w_mix]
        + [query_rows, pairs, chances, normed_all, gain_attn, w_qkv],
        12 * keys * width * width + 4 * count * keys * width * 4,
        raw_outs=2 * parts,
        near=1,
    )
    even, results = results[: -2 * parts], results[-2 * parts :]
    results, returned = lax.optimization_barrier((results, returned))
    odd = permute(odd, "dp", 1)
    held = {2 * i: add(v, odd[i]) for i, v in enumerate(even)}
    for bit in bits_of(dp_size)[1:]:
        for k in [k for k in held if not k & bit]:
            held[k] = add(held[k], permute(held.pop(k | bit).astype(bf16), "dp", bit))
    grad_prompt = held[0]
    (grad_input,) = call(
        finish_kernel,
        [like((count, width), f32)],
        [],
        [block_input, gain_attn, grad_hidden, grad_prompt, grad_rest],
        10 * count * width,
    )
    (output,) = call(
        combine_kernel,
        [like((count, width), bf16)],
        [],
        [hidden, gates, pos, returned],
        4 * slots * count * width,
    )
    grad_up, grad_down = (grads[i : i + 1].astype(f32) for i in range(2))
    first = [grad_input, output, grad_up, grad_down]
    halves, first = sum_blocks([results[2 * i : 2 * i + 2] for i in range(parts)], first)
    grad_input, output, grad_up, grad_down = first
    grad_one, grad_two, grad_router, grad_table, grad_w, grad_mix = call(
        functools.partial(unpack_kernel, experts, heads),
        [like((width,), f32), like((width,), f32), like((experts, width), f32)]
        + [like((heads, 32), f32), like((width, 3 * width), f32), like((width, width), f32)],
        [
            pltpu.VMEM((parts, blocks, width // blocks + 16, part_width), bf16),
            pltpu.VMEM((width, 4 * width), f32),
            pltpu.VMEM((blocks, 8, part_width), f32),
            sems((parts, 2)),
            sems((2, blocks)),
        ],
        halves,
        0,
        raw=2 * parts,
        raw_outs=2,
        limit=28,
    )
    return (
        output,
        grad_input,
        grad_one,
        grad_w,
        grad_mix,
        grad_table.T,
        grad_two,
        grad_router.T,
        grad_up,
        grad_down,
    )


def solution(mesh):
    in_specs = (
        P(("dp", "expert"), None),
        P(),
        P(),
        P(),
        P(),
        P(),
        P(),
        P("expert", None, "dp"),
        P("expert", None, "dp"),
        P(("dp", "expert"), None),
        P(("dp", "expert"), None),
        P(("dp", "expert"), None),
    )
    out_specs = (
        P(("dp", "expert"), None),
        P(("dp", "expert"), None),
        P(),
        P(),
        P(),
        P(),
        P(),
        P(),
        P("expert", None, "dp"),
        P("expert", None, "dp"),
    )
    return jax.shard_map(body, mesh=mesh, in_specs=in_specs, out_specs=out_specs, check_vma=False)
```

```python
import functools
import math

import jax
import jax.numpy as jnp
from jax import lax
from jax.experimental import pallas as pl
from jax.experimental.pallas import tpu as pltpu
from jax.sharding import PartitionSpec as P

CLEN = 128
P_DEV = 128

epsilon = 1e-06
masked_score = -1e30
bucket_edges = [int(math.ceil(16 * 8 ** (step / 16))) for step in range(1, 16)]
bf16 = jnp.bfloat16
f32 = jnp.float32


def contract(left, right, left_dim, right_dim):
    dims = (((left_dim,), (right_dim,)), ((), ()))
    return lax.dot_general(left, right, dims, preferred_element_type=f32)


def dot(left, right):
    return contract(left, right, 1, 0)


def dot_cols(left, right):
    return contract(left, right, 1, 1)


def dot_rows(left, right):
    return contract(left, right, 0, 0)


def iota(shape, axis):
    return lax.broadcasted_iota(jnp.int32, shape, axis)


def like(shape, dtype):
    return jax.ShapeDtypeStruct(shape, dtype)


class Load:
    def __init__(self, source, into, sem):
        self.into = into
        self.copy = pltpu.make_async_copy(source, into, sem)
        self.started = self.waited = False

    def start(self):
        if not self.started:
            self.copy.start()
            self.started = True

    def __call__(self):
        self.start()
        if not self.waited:
            self.copy.wait()
            self.waited = True
        return self.into


class Near:
    def __init__(self, ref):
        self.into = ref

    def __call__(self):
        ref = self.into
        return ref[...].reshape(1, ref.shape[0]) if len(ref.shape) == 1 else ref


def start(*loads):
    for load in loads:
        if isinstance(load, Load):
            load.start()


class Store:
    def __init__(self, ref, into, sems):
        self.ref, self.into, self.sems = ref, into, sems
        self.copies = []

    def send(self, *pieces):
        if not pieces:
            copies = [pltpu.make_async_copy(self.ref, self.into, self.sems.at[0])]
        else:
            copies = [
                pltpu.make_async_copy(self.ref.at[i], self.into.at[i], self.sems.at[at])
                for at, i in enumerate(pieces, len(self.copies))
            ]
        for copy in copies:
            copy.start()
        self.copies += copies

    def begin(self, piece):
        pltpu.make_async_copy(self.ref.at[piece], self.into.at[piece], self.sems.at[piece]).start()

    def begun(self):
        self.copies += [
            pltpu.make_async_copy(self.ref.at[i], self.into.at[i], self.sems.at[i])
            for i in range(self.ref.shape[0])
        ]

    def send_part(self, index, *part):
        source, into = self.ref.at[part], self.into.at[part]
        self.copies.append(pltpu.make_async_copy(source, into, self.sems.at[index]))
        self.copies[-1].start()


def call(body, outs, scratch, args, flops, raw=0, raw_outs=0, near=0, limit=58):
    args, outs = list(args), list(outs)
    count, results = len(args), len(outs)
    flat = [a.ndim == 1 or i < near for i, a in enumerate(args)]
    moved = [i for i in range(count - raw) if not flat[i]]
    direct = [len(o.shape) == 1 or i >= results - raw_outs for i, o in enumerate(outs)]
    pieces = 32

    def kernel(*refs):
        given, refs = refs[:count], refs[count:]
        made, refs = refs[:results], refs[results:]
        held, refs = refs[: len(moved)], refs[len(moved) :]
        ready, refs = refs[: results - sum(direct)], refs[results - sum(direct) :]
        in_sems, out_sems, *rest = refs
        loads = []
        for i in range(count):
            if i in moved:
                at = moved.index(i)
                loads.append(Load(given[i], held[at], in_sems.at[at]))
            elif flat[i]:
                loads.append(Near(given[i]))
            else:
                loads.append(given[i])
        ready = iter(ready)
        stores = [
            made[i] if direct[i] else Store(next(ready), made[i], out_sems.at[i])
            for i in range(results)
        ]
        body(loads, stores, *rest)
        for load in loads:
            if isinstance(load, Load):
                load()
        stores = [store for store in stores if isinstance(store, Store)]
        for store in stores:
            if not store.copies:
                store.send()
        for store in stores:
            for copy in store.copies:
                copy.wait()

    held = [args[i] for i in moved] + [o for o, is_direct in zip(outs, direct) if not is_direct]
    sems = pltpu.SemaphoreType.DMA
    size = sum(math.prod(a.shape) * a.dtype.itemsize for a in args + outs)
    room = [pltpu.VMEM(a.shape, a.dtype) for a in held]
    made = pl.pallas_call(
        kernel,
        out_shape=outs,
        in_specs=[pl.BlockSpec(memory_space=pltpu.VMEM if f else pl.ANY) for f in flat],
        out_specs=[
            pl.BlockSpec(memory_space=pltpu.VMEM if len(o.shape) == 1 else pl.ANY) for o in outs
        ],
        scratch_shapes=room + [sems((max(len(moved), 1),)), sems((results, pieces))] + scratch,
        compiler_params=pltpu.CompilerParams(vmem_limit_bytes=limit << 20),
        cost_estimate=pl.CostEstimate(flops=flops, bytes_accessed=size, transcendentals=0),
    )(*args)
    return list(made)


def bucket_of(distance):
    beyond = sum(((distance >= edge).astype(jnp.int32) for edge in bucket_edges))
    return jnp.clip(jnp.where(distance < 16, distance, 16 + beyond), 0, 31)


def thirds(value):
    high = value.astype(bf16).astype(f32)
    mid = (value - high).astype(bf16).astype(f32)
    return high, mid, value - high - mid


def pieces_of(value, count=3):
    return [v.astype(bf16) for v in thirds(value)[:count]]


def norm_rows(values):
    return lax.rsqrt(jnp.mean(values * values, axis=-1, keepdims=True) + epsilon)


def columns_of(lines):
    count = lines[0].shape[1]
    lines = [line.astype(f32) for line in lines]
    lines += [jnp.zeros((8 - len(lines), count), f32)]
    columns = jnp.transpose(jnp.concatenate(lines, axis=0))
    return [columns[:, c : c + 1] for c in range(len(lines) - 1)]


def route_kernel(experts, cap, rows, loads, stores):
    routes, fill_order, grad_out = loads
    pos, sent = stores
    start(*loads)
    routes = routes()[...]
    count = routes.shape[1]
    order = jnp.broadcast_to(fill_order()[...], (16, 2 * count))
    coarse = order & ~31
    order = jnp.where(iota(order.shape, 0) < 8, coarse, order - coarse).astype(f32).astype(bf16)
    at, to = iota((2 * count, 2 * count), 0), iota((2 * count, 2 * count), 1)
    pick = (at == jnp.where(to < count, 2 * to, 2 * (to - count) + 1)).astype(f32).astype(bf16)
    order = dot(order, pick)
    order = order[:8] + order[8:]
    orow = [order[:1, :count], order[:1, count:]]
    row = [routes[c : c + 1, :].astype(f32) for c in range(2)]
    col = columns_of([*row, *orow])
    col, ocol = col[:2], col[2:]
    slots = []
    for c in range(2):
        rank = jnp.zeros((1, count), f32)
        for other in range(2):
            hit = (col[other] == row[c]) & (ocol[other] < orow[c])
            rank += jnp.sum(hit.astype(f32), axis=0, keepdims=True)
        rank = rank.astype(jnp.int32)
        slot = routes[c : c + 1, :] * rows + rank
        slots.append(jnp.where(rank < cap, slot, -1))
    pos.ref[...] = jnp.concatenate([*slots, jnp.zeros((6, count), jnp.int32)], axis=0)
    pos.send()
    grad_top = grad_out()[...]
    for k in range(experts):
        index = iota((rows, count), 0) + k * rows
        onehot = ((index == slots[0]) | (index == slots[1])).astype(f32).astype(bf16)
        at = slice(k * rows, (k + 1) * rows)
        sent.ref[at, :] = dot(onehot, grad_top).astype(bf16)
        sent.send_part(k, at)


def bias_tiles(table, tiles):
    heads, buckets = table.shape
    width = 2 * P_DEV
    onehot = (bucket_of(iota((buckets, width), 1)) == iota((buckets, width), 0)).astype(f32)
    line = sum(dot(part, onehot.astype(bf16)) for part in pieces_of(table))
    causal = iota((P_DEV, P_DEV), 1) >= iota((P_DEV, P_DEV), 0)
    for h in range(heads):
        spread = jnp.broadcast_to(line[h : h + 1, :], (P_DEV, width))
        rolled = pltpu.roll(spread, 0, 1, stride=1, stride_axis=0)
        tiles[h, 0] = jnp.full((P_DEV, P_DEV), masked_score, f32)
        tiles[h, 1] = jnp.where(causal, rolled[:, :P_DEV], masked_score)
        tiles[h, 2] = rolled[:, P_DEV:]
        tiles[h, 3] = jnp.broadcast_to(line[h : h + 1, width - 1 : width], (P_DEV, P_DEV))


def tile_index(block, dp_size, dp_index, continuation):
    if block == 0:
        return 1 if continuation else 0
    key = dp_index ^ (block - 1)
    if continuation:
        return jnp.minimum(dp_size - key, 2) + 1
    if block == 1:
        return 1
    return jnp.clip(dp_index - key, -1, 2) + 1


def attend_kernel(dp_size, heads, cap, rows, experts, loads, stores, tiles, scores):
    x, *others, w_qkv, gain, table, w_mix, gain_ffn, router, routes, pos = loads
    hidden, kept, gates, chances, pairs, query_rows, normed_all, sent = stores
    start(x, table, *others, w_qkv)
    count, width = x.into.shape
    head_size = width // heads
    dp_index = lax.axis_index("dp")
    values = x()[...].astype(f32)
    low = values * norm_rows(values) * gain()
    normed_all.ref[0:CLEN, :] = low[P_DEV:].astype(bf16)
    normed_all.ref[CLEN:count, :] = low[:P_DEV].astype(bf16)
    for k, other in enumerate(others):
        values = other()[...].astype(f32)
        at = slice((k + 2) * P_DEV, (k + 3) * P_DEV)
        normed_all.ref[at, :] = (values * norm_rows(values) * gain()).astype(bf16)
    normed_all.send()
    bias_tiles(table()[...], tiles)
    pairs, queries, chance = pairs, query_rows.ref, chances.ref
    weights = w_qkv()
    start(w_mix, router, routes, pos)
    queries[...] = dot(normed_all.ref[:count, :], weights[:, :width]).astype(bf16)
    query_rows.send()
    pairs.ref[...] = dot(normed_all.ref[...], weights[:, width:]).astype(bf16)
    pairs.send()
    left = iota((count, P_DEV), 1) < head_size
    for p in range(heads // 2):
        cut = slice(p * P_DEV, (p + 1) * P_DEV)
        key = pairs.ref[:, cut]
        value_t = jnp.transpose(pairs.ref[:, width + p * P_DEV : width + (p + 1) * P_DEV])
        query = queries[:, cut] * bf16(head_size**-0.5)
        zero = jnp.zeros_like(query)
        parts = []
        for s in range(2):
            h = 2 * p + s
            part = jnp.where(left, query, zero) if s == 0 else jnp.where(left, zero, query)
            raw = dot_cols(key, part)
            top = None
            for b in range(dp_size + 1):
                bias = jnp.concatenate(
                    [
                        tiles[h, tile_index(b, dp_size, dp_index, True)],
                        tiles[h, tile_index(b, dp_size, dp_index, False)],
                    ],
                    axis=1,
                )
                block = raw[b * P_DEV : (b + 1) * P_DEV, :] + bias
                scores[s, b * P_DEV : (b + 1) * P_DEV, :] = block
                most = jnp.max(block, axis=0, keepdims=True)
                top = most if top is None else jnp.maximum(top, most)
            total = jnp.zeros((1, count), f32)
            for b in range(dp_size + 1):
                weight = jnp.exp(scores[s, b * P_DEV : (b + 1) * P_DEV, :] - top)
                scores[s, b * P_DEV : (b + 1) * P_DEV, :] = weight
                total += jnp.sum(weight, axis=0, keepdims=True)
            inverse = 1.0 / total
            chance[h, :, :] = (scores[s] * inverse).astype(bf16)
            parts.append(dot(value_t[s * head_size : (s + 1) * head_size, :], chance[h]))
        part = jnp.transpose(jnp.concatenate(parts, axis=0))
        kept.ref[P_DEV:, cut] = part[:CLEN]
        kept.ref[:P_DEV, cut] = part[CLEN:]
        chances.send(2 * p, 2 * p + 1)
    kept.send()
    hid = x()[...].astype(f32) + dot(kept.ref[...].astype(bf16), w_mix()[...])
    hidden.ref[...] = hid
    hidden.send()
    normed_two = hid * norm_rows(hid) * gain_ffn()
    weights = jnp.concatenate([v.astype(f32) for v in pieces_of(router()[...])], axis=0).astype(bf16)
    logits = sum(dot_cols(weights, part) for part in pieces_of(normed_two, 2))
    logits = logits[:experts] + logits[experts : 2 * experts] + logits[2 * experts :]
    row = iota(logits.shape, 0)
    routes = routes()[...]
    pick = [
        jnp.sum(jnp.where(row == routes[c : c + 1, :], logits, 0.0), axis=0, keepdims=True)
        for c in range(2)
    ]
    most = jnp.maximum(pick[0], pick[1])
    raised = [jnp.exp(v - most) for v in pick]
    gate = [v / (raised[0] + raised[1]) for v in raised]
    gates.ref[...] = jnp.concatenate([*gate, jnp.zeros((6, count), f32)], axis=0)
    gates.send()
    pos = pos()[...]
    pos_col = columns_of([pos[c : c + 1, :] for c in range(2)])
    pos_col = [v.astype(jnp.int32) for v in pos_col]
    gate = columns_of(gate)
    lane = iota((count, P_DEV), 1)
    low = normed_two.astype(bf16)
    for k in range(experts):
        index = iota((rows, count), 0) + k * rows
        onehot = (index == pos[0:1, :]) | (index == pos[1:2, :])
        block = dot(onehot.astype(f32).astype(bf16), low)
        line = jnp.zeros((1, P_DEV), f32)
        for c in range(2):
            mine = pos_col[c] == lane + k * rows
            line += jnp.sum(jnp.where(mine, gate[c], 0.0), axis=0, keepdims=True)
        line = jnp.concatenate([*thirds(line), jnp.zeros((1, width - 3 * P_DEV), f32)], axis=1)
        at = slice(k * rows, (k + 1) * rows)
        sent.ref[at, :] = jnp.where(iota((rows, width), 0) == cap, line, block).astype(bf16)
        sent.send_part(k, at)


def gelu_parts(value):
    factor = math.sqrt(2 / math.pi)
    square = value * value
    bend = jnp.tanh(factor * value * (1.0 + 0.044715 * square))
    half = 0.5 * (1.0 + bend)
    slope = half + (0.5 * factor) * value * (1.0 - bend * bend) * (1.0 + 0.134145 * square)
    return value * half, slope


def gather_columns(blocks, into, sems):
    width = into.shape[1] // len(blocks)
    return [
        Load(block, into.at[:, i * width : (i + 1) * width], sems.at[i])
        for i, block in enumerate(blocks)
    ]


def early_kernel(loads, stores, down, early, sems):
    tops, downs = loads
    dp_index = lax.axis_index("dp")
    blocks, width, units = downs.shape
    copies = gather_columns([downs.at[q ^ dp_index] for q in range(blocks)], down, sems.at[0])
    sent = []
    start(tops, *copies[:2])
    for q in range(blocks):
        at = slice(q * units, (q + 1) * units)
        copies[q]()
        start(*copies[q + 1 : q + 3])
        early[q] = dot(tops()[...], down[:, at]).astype(bf16)
        sent.append(pltpu.make_async_copy(early.at[q], stores[0].at[q], sems.at[1, q]))
        sent[-1].start()
    for copy in sent:
        copy.wait()


def payload_line(block, cap, index):
    rows = block.shape[0]
    line = block[rows - 16 :, index * P_DEV : (index + 1) * P_DEV].astype(f32)
    return line[cap - rows + 16 : cap - rows + 17, :]


def gate_column(block, cap):
    line = sum(payload_line(block, cap, i) for i in range(3))
    same = iota((block.shape[0], P_DEV), 0) == iota((block.shape[0], P_DEV), 1)
    return jnp.sum(jnp.where(same, line, 0.0), axis=1, keepdims=True)


def expert_kernel(cap, rows, blocks, loads, stores, up, early, total, product, active, grad_pre, sems):
    got = loads[0]
    back, *kept = stores
    slots, width = got.into.shape
    units = up.shape[1] // blocks
    start(got)

    def fetch(q):
        cut = slice(q * units, (q + 1) * units)
        pltpu.make_async_copy(loads[1 + q], up.at[:, cut], sems.at[0, q]).start()
        pltpu.make_async_copy(loads[-1].at[q], early.at[q], sems.at[1, q]).start()

    fetch(0)
    pieces = [slice(at, at + rows) for at in range(0, slots, rows)]
    same = iota((rows, P_DEV), 0) == iota((rows, P_DEV), 1)
    gates = [gate_column(got()[at, :], cap) for at in pieces]
    chunk = product.shape[2]
    total[...] = jnp.zeros_like(total)
    def step(q, carry):
        base = pl.multiple_of(q*units, units)
        pltpu.make_async_copy(loads[1], up.at[:, pl.ds(base, units)], sems.at[0,q]).wait()
        pltpu.make_async_copy(loads[-1].at[q], early.at[q], sems.at[1,q]).wait()
        for after_q in range(1, blocks):
            pl.when(q + 1 == after_q)(functools.partial(fetch, after_q))
        for i in range(units//chunk):
            to = pl.ds(pl.multiple_of(base + i*chunk, chunk), chunk)
            product[i % 2] = dot(got()[...], up[:, to])
            for at, gate in zip(pieces, gates):
                low, slope = gelu_parts(product[i % 2, at, :])
                active[at, to] = low.astype(bf16)
                grad = early[q, at, i * chunk : (i + 1) * chunk].astype(f32)
                both = grad * low
                total[at, :] += sum(both[:, j : j + P_DEV] for j in range(0, chunk, P_DEV))
                grad_pre[at, to] = (grad * slope * gate).astype(bf16)
        for i, part in enumerate((active, grad_pre)):
            pltpu.make_async_copy(part.at[:, pl.ds(base, units)], kept[i].at[q], sems.at[2 + i, q]).start()
        return carry
    lax.fori_loop(0, blocks, step, 0)
    half = len(pieces) // 2 * rows
    value = [dot_cols(grad_pre[i : i + half, :], up[...]) for i in (0, half)]
    for k, at in enumerate(pieces):
        line = jnp.sum(total[at, :], axis=1, keepdims=True)
        line = jnp.sum(jnp.where(same, line, 0.0), axis=0, keepdims=True)
        line = [*thirds(line), jnp.zeros((1, width - 3 * P_DEV), f32)]
        line = jnp.concatenate(line, axis=1)
        part = value[at.start // half][at.start % half :][:rows]
        back.ref[at, :] = jnp.where(iota((rows, width), 0) == cap, line, part).astype(bf16)
        back.send_part(k, at)
    for q in range(blocks):
        for i, part in enumerate((active, grad_pre)):
            pltpu.make_async_copy(part.at[:, q*units:(q+1)*units], kept[i].at[q], sems.at[2 + i, q]).wait()

def weight_kernel(cap, rows, blocks, loads, stores, grad_pre, active, down, sems):
    got, tops, *whole, downs = loads
    dp_index = lax.axis_index("dp")
    start(got, tops)
    units = active.shape[1] // blocks

    def copies_of(q):
        cut = pl.ds(pl.multiple_of(q * units, units), units)
        sources = (whole[0].at[q], whole[1].at[q], downs.at[q ^ dp_index])
        return [
            pltpu.make_async_copy(source, into.at[:, cut], sems.at[i, q])
            for i, (source, into) in enumerate(zip(sources, (grad_pre, active, down)))
        ]

    for q in range(blocks):
        for copy in copies_of(q):
            copy.start()
    grads, result = stores
    grad_out = []
    for at in range(0, got.into.shape[0], rows):
        gate = gate_column(got()[at : at + rows, :], cap)
        grad_out.append((gate * tops()[at : at + rows, :].astype(f32)).astype(bf16))
    rows_t = jnp.transpose(got()[...])
    grad_t = jnp.transpose(jnp.concatenate(grad_out, axis=0))

    def step(q, carry):
        for copy in copies_of(q):
            copy.wait()
        cut = pl.ds(pl.multiple_of(q * units, units), units)
        grads.ref[q ^ dp_index, 0] = dot(rows_t, grad_pre[:, cut]).astype(bf16)
        grads.ref[q ^ dp_index, 1] = dot(grad_t, active[:, cut]).astype(bf16)
        grads.begin(q ^ dp_index)
        return carry

    lax.fori_loop(0, blocks, step, 0)
    grads.begun()
    result.ref[...] = dot_cols(active[...], down[...]).astype(bf16)


def combine_kernel(loads, stores):
    hidden, gates, pos, back = loads
    (output,) = stores
    start(*loads)
    columns = columns_of([gates()[0:1, :], gates()[1:2, :], pos()[0:1, :], pos()[1:2, :]])
    held = back()[...]
    index = iota((hidden.into.shape[0], held.shape[0]), 1)
    total = hidden()[...]
    for c in range(2):
        onehot = (index == columns[2 + c].astype(jnp.int32)).astype(f32).astype(bf16)
        total += columns[c] * dot(onehot, held)
    output.ref[...] = total.astype(bf16)


def diagonal_sums(values):
    size, width = values.shape
    while size > 8:
        size //= 2
        values = values[:size] + pltpu.roll(values[size:], width - size, 1)
    row = iota(values.shape, 0)
    for bit in (4, 2, 1):
        values = jnp.where((row & bit) != 0, pltpu.roll(values, width - bit, 1), values)
    return jnp.sum(values, axis=0, keepdims=True)


def backward_kernel(dp_size, heads, cap, loads, stores, grad_att, delta, sums, grad_query,
                    grad_pairs, normed_t, lines, staged, sems):
    back, hidden, gates, pos, routes, gain_ffn, router, grad_output, kept, w_mix = loads[:10]
    query_rows, pairs, chances, normed_all, gain, w_qkv = loads[10:]
    start(back, gates, pos, routes, hidden, router, grad_output, kept, w_mix)
    experts = router.into.shape[0]
    rows = back.into.shape[0] // experts
    (grad_hidden, grad_rest, grad_odd), stores = stores[:3], stores[3:]
    parts = staged.shape[0]
    grad_even, halves = stores[: -2 * parts], stores[-2 * parts :]
    mine = [block_index(order) for order in orders]
    width = hidden.into.shape[1]
    blocks, step_rows, part_width = staged.shape[1], width // staged.shape[1], staged.shape[3]
    copies = []

    def put(first, value):
        for at in range(0, value.shape[1], 256):
            index, into = divmod(first + at, part_width)
            for p in range(blocks):
                part = value[p * step_rows : (p + 1) * step_rows, at : at + 256]
                to = slice(into, into + 256)
                staged[index, p ^ mine[index], 0:step_rows, to] = part.astype(bf16)

    def send(index, small=()):
        half = blocks // 2
        count = step_rows + (16 if small else 0)
        for p in range(blocks if small else 0):
            more = small[p] if p < len(small) else jnp.zeros((8, width), f32)
            more = jnp.concatenate([more, jnp.zeros_like(more)], axis=0)
            staged[index, p ^ mine[index], step_rows:, 0:width] = more.astype(bf16)
        for i in range(2):
            source = staged.at[index, i * half : (i + 1) * half, 0:count]
            into = halves[2 * index + i]
            copies.append(pltpu.make_async_copy(source, into, sems.at[index, i]))
            copies[-1].start()

    count, width = hidden.into.shape
    head_size = width // heads
    given = [gates()[0:1, :], gates()[1:2, :]]
    given += [ref[c : c + 1, :] for ref in (pos(), routes()) for c in range(2)]
    columns = columns_of(given)
    gate = columns[:2]
    pos, routes = ([v.astype(jnp.int32) for v in columns[i : i + 2]] for i in (2, 4))
    index = iota((count, experts * rows), 1)
    onehot = (index == pos[0]) | (index == pos[1])
    grad_two = dot(onehot.astype(f32).astype(bf16), back()[...])
    lane = iota((count, P_DEV), 1)
    found = [jnp.zeros((count, P_DEV), f32) for c in range(2)]
    for k in range(experts):
        line = sum(payload_line(back()[k * rows : (k + 1) * rows, :], cap, i) for i in range(3))
        for c in range(2):
            found[c] += jnp.where(pos[c] == lane + k * rows, line, 0.0)
    grad_gate = [jnp.sum(v, axis=1, keepdims=True) for v in found]
    hid = hidden()[...]
    start(query_rows, pairs, chances)
    scale = norm_rows(hid)
    normed_two = hid * scale * gain_ffn()
    slope = gate[0] * gate[1] * (grad_gate[0] - grad_gate[1])
    lane = iota((count, experts), 1)
    grad_logits = jnp.where(lane == routes[0], slope, 0.0) - jnp.where(lane == routes[1], slope, 0.0)
    left = thirds(grad_logits)
    right = thirds(router()[...])
    pairs_of = [(0, 0), (0, 1), (1, 0), (0, 2), (1, 1), (2, 0)]
    left_all = jnp.concatenate([left[i] for i, _ in pairs_of], axis=1).astype(bf16)
    right_all = jnp.concatenate([right[i] for _, i in pairs_of], axis=0).astype(bf16)
    grad_two += dot(left_all, right_all)
    left = jnp.transpose(jnp.concatenate(left, axis=1)).astype(bf16)
    grad_router = sum(dot(left, part) for part in pieces_of(normed_two, 2))
    grad_router = grad_router[:experts] + grad_router[experts : 2 * experts] + grad_router[2 * experts :]
    grad_gain_ffn = jnp.sum(grad_two * hid * scale, axis=0, keepdims=True)
    weighted = grad_two * gain_ffn()
    inner = jnp.mean(weighted * hid, axis=-1, keepdims=True)
    grad_hid = grad_output()[...].astype(f32) + scale * weighted - hid * (scale**3 * inner)
    grad_hidden.ref[...] = grad_hid
    grad_hidden.send()
    mixed = grad_hid.astype(bf16)
    att = kept()[...]
    weights = w_mix()[...]
    start(normed_all, w_qkv)
    top = dot_cols(mixed, weights).astype(bf16)
    grad_att[0:CLEN, :] = top[P_DEV:]
    grad_att[CLEN:, :] = top[:P_DEV]
    put(3 * width, dot_rows(att.astype(bf16), mixed))
    prod_t = jnp.transpose(top.astype(f32) * att)
    for h in range(heads):
        line = prod_t[h * head_size : (h + 1) * head_size, :]
        line = jnp.sum(line, axis=0, keepdims=True)
        delta[h : h + 1, :] = jnp.concatenate([line[:, P_DEV:], line[:, :P_DEV]], axis=1)
    dp_index = lax.axis_index("dp")
    left = iota((count, P_DEV), 1) < head_size
    left_keys = iota((pairs.into.shape[0], P_DEV), 1) < head_size
    lines[...] = jnp.zeros_like(lines)
    queries, pairs_ref, chances = query_rows(), pairs(), chances()
    for p in range(heads // 2):
        cut = slice(p * P_DEV, (p + 1) * P_DEV)
        cut_value = slice(width + p * P_DEV, width + (p + 1) * P_DEV)
        key_t = jnp.transpose(pairs_ref[:, cut])
        value = pairs_ref[:, cut_value]
        query = queries[:, cut] * bf16(head_size**-0.5)
        top = grad_att[:, cut]
        zero = jnp.zeros_like(top)
        grad_q, grad_k, grad_v = [], [], []
        for s in range(2):
            h = 2 * p + s
            part = jnp.where(left, top, zero) if s == 0 else jnp.where(left, zero, top)
            grad_chance = dot_cols(value, part)
            chance = chances[h]
            grad_score = (chance.astype(f32) * (grad_chance - delta[h : h + 1, :])).astype(bf16)
            grad_v.append(dot(chance, top))
            grad_k.append(dot(grad_score, query))
            grad_q.append(dot(key_t[s * head_size : (s + 1) * head_size, :], grad_score))
            sums[...] = jnp.zeros_like(sums)
            for b in range(dp_size + 1):
                tile = grad_score[b * P_DEV : (b + 1) * P_DEV, :].astype(f32)
                sums[tile_index(b, dp_size, dp_index, True)] += tile[:, :P_DEV]
                if b > 0:
                    sums[tile_index(b, dp_size, dp_index, False)] += tile[:, P_DEV:]
            both = jnp.concatenate([sums[1], sums[2]], axis=1)
            lines[h : h + 1, : 2 * P_DEV] = diagonal_sums(both)
            lines[h : h + 1, 2 * P_DEV :] = jnp.sum(sums[3], axis=0, keepdims=True)
        grad_pairs[:, cut] = jnp.where(left_keys, grad_k[0], grad_k[1]).astype(bf16)
        grad_pairs[:, cut_value] = jnp.where(left_keys, grad_v[0], grad_v[1]).astype(bf16)
        grad_q = jnp.transpose(jnp.concatenate(grad_q, axis=0) * head_size**-0.5)
        grad_query[:, cut] = grad_q.astype(bf16)
    normed_all = normed_all()
    normed_t[...] = jnp.transpose(normed_all[...])
    w_qkv = w_qkv()
    grad_low = dot_cols(grad_pairs[...], w_qkv[:, width:])
    for k in range(1, dp_size):
        part = grad_low[(k + 1) * P_DEV : (k + 2) * P_DEV].astype(bf16)
        if k % 2:
            grad_odd.ref[k // 2] = part
        else:
            grad_even[k // 2].ref[...] = part
            grad_even[k // 2].send()
    grad_odd.send()
    own = grad_low[:count] + dot_cols(grad_query[...], w_qkv[:, :width])
    grad_rest.ref[...] = own[:CLEN]
    grad_rest.send()
    grad_even[0].ref[...] = own[CLEN:]
    grad_even[0].send()
    grad_gain = jnp.sum(own * normed_all[:count, :].astype(f32), axis=0, keepdims=True)
    grad_gain += jnp.sum(
        grad_low[count:] * normed_all[count:, :].astype(f32), axis=0, keepdims=True
    )
    grad_gain = grad_gain / gain()
    distance = iota((lines.shape[1], P_DEV), 0)
    bucket = jnp.where(distance < 2 * P_DEV, bucket_of(distance), 31)
    onehot = (bucket == iota((lines.shape[1], P_DEV), 1)).astype(f32).astype(bf16)
    table = sum(dot(part, onehot) for part in pieces_of(lines[...]))
    table = jnp.concatenate([table, jnp.zeros((16, width - P_DEV), f32)], axis=1)
    row = iota((8, width), 0)
    small = [jnp.where(row == 0, grad_gain, jnp.where(row == 1, grad_gain_ffn, 0.0))]
    small += [table[:8], table[8:]]
    small += [grad_router[i : i + 8] for i in range(0, experts, 8)]
    put(0, dot(normed_t[:, :count], grad_query[...]))
    put(width, dot(normed_t[...], grad_pairs[:, :width]))
    send(0)
    put(2 * width, dot(normed_t[...], grad_pairs[:, width:]))
    send(1)
    send(2, small)
    for copy in copies:
        copy.wait()


def unpack_kernel(experts, heads, loads, stores, held, staged, small, sems_in, sems):
    gain_one, gain_two, router, table, grad_w, grad_mix = stores
    half, _, part_width = loads[0].shape
    parts = len(loads) // 2
    width, rows = grad_mix.shape[1], staged.shape[0] // (2 * half)
    halves = []
    for index in range(parts):
        count = loads[2 * index].shape[1]
        for j in range(2):
            into = held.at[index, j * half : (j + 1) * half, 0:count]
            halves.append(Load(loads[2 * index + j], into, sems_in.at[index, j]))
    start(*halves[0::2], *halves[1::2])
    mine = [block_index(order) for order in orders]
    copies = []
    for j in range(2 * half):
        if j % half == 0:
            for load in halves[j // half :: 2]:
                load()
        p = j ^ (mine[0] // half * half)
        at = pl.ds(pl.multiple_of(p * rows, rows), rows)
        to = slice(j * rows, (j + 1) * rows)
        for index in range(parts):
            place = j // half * half + ((j ^ mine[index]) % half)
            block = held[index, place].astype(f32)
            staged[to, index * part_width : (index + 1) * part_width] = block[:rows]
        small[p] = block[rows : rows + 8]
        for i, into in enumerate((grad_w, grad_mix)):
            cut = slice(0, 3 * width) if i == 0 else slice(3 * width, 4 * width)
            copies.append(pltpu.make_async_copy(staged.at[to, cut], into.at[at], sems.at[i, j]))
            copies[-1].start()
    gain_one[...] = small[0, 0, :width]
    gain_two[...] = small[0, 1, :width]
    lines = jnp.concatenate([small[1], small[2]], axis=0)
    table.ref[...] = lines[:heads, :32]
    for i in range(experts // 8):
        router.ref[i * 8 : (i + 1) * 8, :] = small[3 + i][:, :width]
    for copy in copies:
        copy.wait()


def finish_kernel(loads, stores):
    x, gain, grad_hidden, grad_prompt, grad_rest = loads
    start(*loads)
    values = x()[...].astype(f32)
    scale = norm_rows(values)
    grad = jnp.concatenate([grad_prompt()[...], grad_rest()[...]], axis=0)
    weighted = grad * gain()
    inner = jnp.mean(weighted * values, axis=-1, keepdims=True)
    stores[0].ref[...] = grad_hidden()[...] + scale * weighted - values * (scale**3 * inner)


def permute(value, axis, offset):
    size = lax.axis_size(axis)
    return lax.ppermute(value, axis, [(i, i ^ offset) for i in range(size)])


def bits_of(size):
    return [1 << b for b in range(size.bit_length() - 1)]


def spread_far(block):
    held = {0: block}
    for bit in bits_of(lax.axis_size("dp"))[:0:-1]:
        held.update({k ^ bit: permute(v, "dp", bit) for k, v in list(held.items())})
    return held


def spread_near(held):
    held = held | {k ^ 1: permute(v, "dp", 1) for k, v in held.items()}
    return [held[k] for k in sorted(held)]


def swap(blocks):
    return lax.all_to_all(blocks, "expert", split_axis=0, concat_axis=0, tiled=True)


def add(left, right):
    return left.astype(f32) + right.astype(f32)


def after(value, *first):
    return lax.optimization_barrier((value, *first))[0]


halving = {"c": ("dp", 1), "x": ("dp", 2), "y": ("expert", 1), "z": ("expert", 2)}
orders = ["cyzx", "czyx", "cyzx"]
widening = ["zxy", "xyz", "yzx"]


def block_index(order):
    index = jnp.int32(0)
    for name in order:
        axis, bit = halving[name]
        index = index * 2 + (lax.axis_index(axis) & bit) // bit
    return index


def halve(keep, send, order):
    for name in order[:-1]:
        blocks = add(keep, permute(send, *halving[name])).astype(bf16)
        half = blocks.shape[0] // 2
        keep, send = blocks[:half], blocks[half:]
    return add(keep, permute(send, *halving[order[-1]])).astype(bf16)


def widen(blocks, order, back):
    for name in back:
        more = permute(blocks, *halving[name])
        blocks = jnp.concatenate([blocks, more], axis=order.index(name))
    return blocks


def other_steps():
    return [(axis, bit) for axis in ("dp", "expert") for bit in bits_of(lax.axis_size(axis))
            if (axis, bit) not in halving.values()]


def sum_blocks(parts, first):
    parts = [halve(*part, order) for part, order in zip(parts, orders)]
    whole = jnp.concatenate(parts, axis=1)
    for step in other_steps():
        whole = add(whole, permute(whole, *step)).astype(bf16)
    wide = []
    at = 0
    for part, order, back in zip(parts, orders, widening):
        block = whole[:, at : at + part.shape[1]]
        block = block.reshape((1,) * len(order) + block.shape[1:])
        wide.append(widen(block, order, back[:-1]))
        at += part.shape[1]
    wide[-1], first = lax.optimization_barrier((wide[-1], first))
    halves = []
    for block, order, back in zip(wide, orders, widening):
        block = widen(block, order, back[-1:])
        block = block.reshape(-1, *block.shape[-2:])
        halves += [block, permute(block, *halving[order[0]])]
    return halves, first


def body(
    block_input,
    gain_attn,
    w_qkv,
    w_mix,
    rel_bias,
    gain_ffn,
    w_router,
    w_up,
    w_down,
    routes,
    fill_order,
    grad_output,
):
    count, width = block_input.shape
    heads = rel_bias.shape[1]
    dp_size = lax.axis_size("dp")
    experts = w_router.shape[1]
    cap = 9 * 2 * count // (8 * experts)
    rows = (cap + 16) // 16 * 16
    slots = experts * rows
    keys = (dp_size + 1) * P_DEV
    units = w_up.shape[2]
    hidden_units = units * dp_size
    routes, router = routes.T, w_router.T
    packed = like((slots, width), bf16)

    others = spread_far(block_input[:P_DEV])
    downs = lax.all_gather(w_down[0], "dp", axis=0)
    pos, tops = call(
        functools.partial(route_kernel, experts, cap, rows),
        [like((8, count), jnp.int32), packed],
        [],
        [routes, fill_order, grad_output],
        2 * slots * count * width,
    )
    tops, others = lax.optimization_barrier((tops, others))
    tops = swap(tops)
    others = spread_near(others)[1:]
    hidden, kept, gates, chances, pairs, query_rows, normed_all, sent = call(
        functools.partial(attend_kernel, dp_size, heads, cap, rows, experts),
        [
            like((count, width), f32),
            like((count, width), f32),
            like((8, count), f32),
            like((heads, keys, count), bf16),
            like((keys, 2 * width), bf16),
            like((count, width), bf16),
            like((keys, width), bf16),
            packed,
        ],
        [
            pltpu.VMEM((heads, 4, P_DEV, P_DEV), f32),
            pltpu.VMEM((2, keys, count), f32),
        ],
        [block_input, *others, w_qkv, gain_attn, rel_bias.T, w_mix, gain_ffn, router]
        + [routes, pos],
        4 * keys * width * width + 4 * count * keys * width * 2,
    )
    sems = pltpu.SemaphoreType.DMA
    (early,) = call(
        early_kernel,
        [like((dp_size, slots, units), bf16)],
        [
            pltpu.VMEM((width, hidden_units), bf16),
            pltpu.VMEM((dp_size, slots, units), bf16),
            sems((2, dp_size)),
        ],
        [tops, downs],
        2 * slots * width * hidden_units,
        raw=1,
        raw_outs=1,
    )
    w_near, w_far, sent = lax.optimization_barrier((w_up, w_up, sent))
    got = swap(sent)
    ups = spread_far(w_far[0])
    del ups[0]
    ups, early = lax.optimization_barrier((ups, early))
    ups |= {k ^ 1: permute(v, "dp", 1) for k, v in ups.items()}
    ups |= {0: w_up[0], 1: permute(w_near[0], "dp", 1)}
    back, active, grad_pre = call(
        functools.partial(expert_kernel, cap, rows, dp_size),
        [packed] + [like((dp_size, slots, units), bf16)] * 2,
        [
            pltpu.VMEM((width, hidden_units), bf16),
            pltpu.VMEM((dp_size, slots, units), bf16),
            pltpu.VMEM((slots, P_DEV), f32),
            pltpu.VMEM((2, slots, 256 if units % 256 == 0 else 128), f32),
            pltpu.VMEM((slots, hidden_units), bf16),
            pltpu.VMEM((slots, hidden_units), bf16),
            sems((4, dp_size)),
        ],
        [got, *(ups[k] for k in range(dp_size)), early],
        4 * slots * width * hidden_units,
        raw=dp_size + 1,
        raw_outs=2,
    )
    back = swap(back)
    grads, result = call(
        functools.partial(weight_kernel, cap, rows, dp_size),
        [like((dp_size, 2, width, units), bf16), packed],
        [pltpu.VMEM((slots, hidden_units), bf16)] * 2
        + [pltpu.VMEM((width, hidden_units), bf16), sems((3, dp_size))],
        [got, tops, grad_pre, active, downs],
        6 * slots * width * hidden_units,
        raw=3,
    )
    grads, result, back = lax.optimization_barrier((grads, result, back))
    grads = lax.psum_scatter(grads, "dp", scatter_dimension=0)
    returned = swap(result)

    blocks = 1 << len(orders[0])
    parts = len(orders)
    part_width = 4 * width // parts
    rows_of = [width // blocks + 16 * (i == parts - 1) for i in range(parts)]
    half = [like((blocks // 2, rows, part_width), bf16) for rows in rows_of for _ in range(2)]
    grad_hidden, grad_rest, odd, *results = call(
        functools.partial(backward_kernel, dp_size, heads, cap),
        [like((count, width), f32), like((CLEN, width), f32)]
        + [like((dp_size // 2, P_DEV, width), bf16), like((P_DEV, width), f32)]
        + [like((P_DEV, width), bf16)] * (dp_size // 2 - 1)
        + half,
        [
            pltpu.VMEM((count, width), bf16),
            pltpu.VMEM((16, count), f32),
            pltpu.VMEM((4, P_DEV, P_DEV), f32),
            pltpu.VMEM((count, width), bf16),
            pltpu.VMEM((keys, 2 * width), bf16),
            pltpu.VMEM((width, keys), bf16),
            pltpu.VMEM((16, 3 * P_DEV), f32),
            pltpu.VMEM((parts, blocks, width // blocks + 16, part_width), bf16),
            sems((parts, 2)),
        ],
        [back, hidden, gates, pos, routes, gain_ffn, router, grad_output, kept, w_mix]
        + [query_rows, pairs, chances, normed_all, gain_attn, w_qkv],
        12 * keys * width * width + 4 * count * keys * width * 4,
        raw_outs=2 * parts,
        near=1,
    )
    even, results = results[: -2 * parts], results[-2 * parts :]
    results, returned = lax.optimization_barrier((results, returned))
    odd = permute(odd, "dp", 1)
    held = {2 * i: add(v, odd[i]) for i, v in enumerate(even)}
    for bit in bits_of(dp_size)[1:]:
        for k in [k for k in held if not k & bit]:
            held[k] = add(held[k], permute(held.pop(k | bit).astype(bf16), "dp", bit))
    grad_prompt = held[0]
    (grad_input,) = call(
        finish_kernel,
        [like((count, width), f32)],
        [],
        [block_input, gain_attn, grad_hidden, grad_prompt, grad_rest],
        10 * count * width,
    )
    (output,) = call(
        combine_kernel,
        [like((count, width), bf16)],
        [],
        [hidden, gates, pos, returned],
        4 * slots * count * width,
    )
    grad_up, grad_down = (grads[i : i + 1].astype(f32) for i in range(2))
    first = [grad_input, output, grad_up, grad_down]
    halves, first = sum_blocks([results[2 * i : 2 * i + 2] for i in range(parts)], first)
    grad_input, output, grad_up, grad_down = first
    grad_one, grad_two, grad_router, grad_table, grad_w, grad_mix = call(
        functools.partial(unpack_kernel, experts, heads),
        [like((width,), f32), like((width,), f32), like((experts, width), f32)]
        + [like((heads, 32), f32), like((width, 3 * width), f32), like((width, width), f32)],
        [
            pltpu.VMEM((parts, blocks, width // blocks + 16, part_width), bf16),
            pltpu.VMEM((width, 4 * width), f32),
            pltpu.VMEM((blocks, 8, part_width), f32),
            sems((parts, 2)),
            sems((2, blocks)),
        ],
        halves,
        0,
        raw=2 * parts,
        raw_outs=2,
        limit=28,
    )
    return (
        output,
        grad_input,
        grad_one,
        grad_w,
        grad_mix,
        grad_table.T,
        grad_two,
        grad_router.T,
        grad_up,
        grad_down,
    )


def solution(mesh):
    in_specs = (
        P(("dp", "expert"), None),
        P(),
        P(),
        P(),
        P(),
        P(),
        P(),
        P("expert", None, "dp"),
        P("expert", None, "dp"),
        P(("dp", "expert"), None),
        P(("dp", "expert"), None),
        P(("dp", "expert"), None),
    )
    out_specs = (
        P(("dp", "expert"), None),
        P(("dp", "expert"), None),
        P(),
        P(),
        P(),
        P(),
        P(),
        P(),
        P("expert", None, "dp"),
        P("expert", None, "dp"),
    )
    return jax.shard_map(body, mesh=mesh, in_specs=in_specs, out_specs=out_specs, check_vma=False)
```
